128 devices in a mesh: row: 32 (over y, x_lo, z), col: 4 (over x_hi, core).
Axes of the slice: x: 4 (x_hi: 2, x_lo: 2; x = x_hi * 2 + x_lo), y: 4, z: 4, core: 2. Of those that a mesh axis runs over, the one named last changes fastest.
Arguments:
- features: bfloat16 [32768, 256], P('row', 'col'), may hold values from -6 to 6
- weight: bfloat16 [256, 256], replicated, may hold values from -0.375 to 0.375
- bias: float32 [256], P('col'), may hold values from -4 to 4
- edge_blocks: bfloat16 [32, 32, 16, 128, 128], P('row'), may hold values from 0.0003528595 to 0.03515625
- block_dst: int32 [32, 32, 16], P('row'), may hold values from 0 to 7
- block_src: int32 [32, 32, 16], P('row'), may hold values from 0 to 7
- counts: int32 [32, 32], P('row'), may hold values from 1 to 16, as said below
- cotangent: bfloat16 [32768, 256], P('row', 'col'), may hold values from -6 to 6
Outputs:
- output: bfloat16 [32768, 256], P('row', 'col')
- grad_input: bfloat16 [32768, 256], P('row', 'col')
- grad_weight: float32 [256, 256], P('col')
- grad_bias: float32 [256], P('col')
The draws below stay inside these ranges and needn't reach their ends.
Inputs may be any that keep to these rules, and one draw needn't show every extreme that they name: `counts`: every panel's pair with itself has all 16 slots live.
All inputs are finite; a program needn't handle non-finite values.
Results may differ from the reference program's by a relative error of at most 0.008.
Values may be sent and summed in bfloat16 or wider, within the bound.
A program may use at most 128 MiB of HBM per device.

```python
import math
import jax
import jax.numpy as jnp
from jax import lax

F = 256
BS = 128
BPAN = 8
KB = 16
P_SIZE = 1024
PANELS = 32
NODES = 32768


def draw_counts(key, part):
    key = jax.random.fold_in(key, 11)
    key_order, key_high, key_low = jax.random.split(key, 3)
    order = jax.random.permutation(key_order, PANELS)
    heavy = order < max(1, PANELS // 4)
    high = jax.random.randint(key_high, (PANELS, PANELS), KB // 2, KB + 1)
    low = jax.random.randint(key_low, (PANELS, PANELS), 1, max(2, KB // 4 + 1))
    chosen = jnp.where(heavy[:, None], high, low)
    diag = jnp.arange(PANELS)[:, None] == jnp.arange(PANELS)[None, :]
    return jnp.where(diag, KB, chosen).astype(jnp.int32)


def set_ends(array, own_key, least, largest):
    dims = array.shape
    spot = [jax.random.randint(jax.random.fold_in(own_key, axis), (), 0, dims[axis]) for axis in range(len(dims))]
    array = array.at[tuple(spot)].set(least)
    longest = dims.index(max(dims))
    spot[longest] = (spot[longest] + 1) % dims[longest]
    return array.at[tuple(spot)].set(largest)


def level_of(own_key, shape, pieces, smallest, largest):
    level, own = 1.0, jax.random.fold_in(own_key, 6)
    for axis_at, parts in pieces:
        draws = jnp.exp(jax.random.uniform(jax.random.fold_in(own, axis_at), (parts,), jnp.float32, smallest / len(pieces), largest / len(pieces)))
        level = level * jnp.repeat(draws, shape[axis_at] // parts).reshape([-1 if axis == axis_at else 1 for axis in range(len(shape))])
    return level


def scatter_about(own_key, dims, scale, bound, cuts=(), held_as=jnp.bfloat16):
    loudness = level_of(own_key, dims, cuts, -0.22, 0.18) if cuts else 1.0
    array = jax.random.normal(own_key, dims, jnp.float32) * scale * loudness
    return jnp.minimum(jnp.maximum(array, -bound), bound).astype(held_as)


def setup_inputs(seed: int = 0) -> dict:
    key_list = jax.random.split(jax.random.key(seed), 9)
    return {
        "features": scatter_about(key_list[0], (NODES, F), 1.0, 6.0, ((0, 32), (1, 4))),
        "weight": scatter_about(key_list[1], (F, F), F ** -0.5, 0.375),
        "bias": scatter_about(key_list[2], (F,), 1.0, 4.0, ((0, 4),), jnp.float32),
        "edge_blocks": jnp.clip(jnp.exp(math.log(0.03515625) - 4.6014877 * jax.random.uniform(key_list[3], (PANELS, PANELS, KB, BS, BS), jnp.float32) ** level_of(key_list[3], (PANELS, PANELS, KB, BS, BS), ((0, 32),), -0.2, 0.2)), 0.0003528595, 0.03515625).astype(jnp.bfloat16),
        "block_dst": set_ends(jax.random.randint(key_list[4], (PANELS, PANELS, KB), 0, BPAN), jax.random.fold_in(key_list[4], 1), 0, BPAN - 1).astype(jnp.int32),
        "block_src": set_ends(jax.random.randint(key_list[5], (PANELS, PANELS, KB), 0, BPAN), jax.random.fold_in(key_list[5], 1), 0, BPAN - 1).astype(jnp.int32),
        "counts": draw_counts(jax.random.fold_in(key_list[8], 71), 0),
        "cotangent": scatter_about(key_list[7], (NODES, F), 1.0, 6.0, ((0, 32), (1, 4))),
    }


def forward_panel(blocks, src_ids, dst_ids, live_k, xpanel):
    size = blocks.shape[-1]
    nblk = xpanel.shape[0] // size
    places = jnp.arange(nblk, dtype=jnp.int32)
    xblock = xpanel.reshape(nblk, size, -1).astype(jnp.float32)
    pick = (src_ids[:, None] == places[None, :]).astype(jnp.float32)
    chosen = jnp.einsum('kb,bnf->knf', pick, xblock, precision=lax.Precision.HIGHEST)
    prods = jnp.einsum('kmn,knf->kmf', blocks.astype(jnp.float32), chosen, precision=lax.Precision.HIGHEST)
    put = ((dst_ids[None, :] == places[:, None]) & live_k[None, :]).astype(jnp.float32)
    return jnp.einsum('bk,kmf->bmf', put, prods, precision=lax.Precision.HIGHEST).reshape(nblk * size, -1)


def adjoint_panel(blocks, src_ids, dst_ids, live_k, gpanel):
    size = blocks.shape[-1]
    nblk = gpanel.shape[0] // size
    places = jnp.arange(nblk, dtype=jnp.int32)
    gblock = gpanel.reshape(nblk, size, -1).astype(jnp.float32)
    pick = ((dst_ids[:, None] == places[None, :]) & live_k[:, None]).astype(jnp.float32)
    chosen = jnp.einsum('kb,bmf->kmf', pick, gblock, precision=lax.Precision.HIGHEST)
    prods = jnp.einsum('kmn,kmf->knf', blocks.astype(jnp.float32), chosen, precision=lax.Precision.HIGHEST)
    put = (src_ids[None, :] == places[:, None]).astype(jnp.float32)
    return jnp.einsum('bk,knf->bnf', put, prods, precision=lax.Precision.HIGHEST).reshape(nblk * size, -1)


def reference(features, weight, bias, edge_blocks, block_dst, block_src, counts, cotangent):
    live = jnp.arange(KB, dtype=jnp.int32)[None, None, :] < counts[:, :, None]
    panels_x = features.reshape(PANELS, P_SIZE, F)

    def dest_panel(i):
        def step(total, j):
            return total + forward_panel(edge_blocks[i, j], block_src[i, j], block_dst[i, j], live[i, j], panels_x[j]), None
        total, _ = lax.scan(step, jnp.zeros((P_SIZE, F), jnp.float32), jnp.arange(PANELS, dtype=jnp.int32))
        return total

    aggregated = lax.map(dest_panel, jnp.arange(PANELS, dtype=jnp.int32)).reshape(NODES, F).astype(jnp.bfloat16)
    pre = jnp.dot(aggregated, weight, preferred_element_type=jnp.float32) + bias
    output = jax.nn.silu(pre).astype(jnp.bfloat16)
    sig = jax.nn.sigmoid(pre)
    grad_pre = (cotangent.astype(jnp.float32) * sig * (1.0 + pre * (1.0 - sig))).astype(jnp.bfloat16)
    grad_agg = jnp.dot(grad_pre, weight.T, preferred_element_type=jnp.float32).astype(jnp.bfloat16)
    panels_g = grad_agg.reshape(PANELS, P_SIZE, F)

    def src_panel(j):
        def step(total, i):
            return total + adjoint_panel(edge_blocks[i, j], block_src[i, j], block_dst[i, j], live[i, j], panels_g[i]), None
        total, _ = lax.scan(step, jnp.zeros((P_SIZE, F), jnp.float32), jnp.arange(PANELS, dtype=jnp.int32))
        return total

    grad_input = lax.map(src_panel, jnp.arange(PANELS, dtype=jnp.int32)).reshape(NODES, F).astype(jnp.bfloat16)
    scale = 1.0 / (NODES ** 0.5)
    grad_weight = jnp.dot(aggregated.T, grad_pre, preferred_element_type=jnp.float32) * scale
    grad_bias = jnp.sum(grad_pre.astype(jnp.float32), axis=0) * scale
    return output, grad_input, grad_weight, grad_bias
```

```python
import functools

import jax
import jax.numpy as jnp
from jax import lax
from jax.experimental import pallas as pl
from jax.experimental.pallas import tpu as pltpu
from jax.sharding import PartitionSpec as P

MESH = pl.DeviceIdType.MESH
BF = jnp.bfloat16
F32 = jnp.float32

YP, YM, ZP, ZM = (1, 0), (-1, 0), (0, 1), (0, -1)


def _message(half, way, dy, dz):
    return (half, way, 4 * dy + dz, 4 * ((dy - way[0]) % 4) + (dz - way[1]) % 4)


ROUNDS = (
    (_message(0, YP, 0, 0), _message(0, YM, 0, 0), _message(1, ZP, 0, 0), _message(1, ZM, 0, 0)),
    (_message(1, YP, 0, 0), _message(1, YM, 0, 0), _message(0, ZP, 0, 0), _message(0, ZM, 0, 0)),
    (_message(0, YP, 3, 0), _message(1, YM, 0, 1), _message(1, ZP, 0, 3), _message(0, ZM, 1, 0)),
    (_message(1, YP, 0, 1), _message(1, YM, 0, 3), _message(0, ZP, 1, 0), _message(0, ZM, 3, 0)),
    (_message(1, YP, 0, 3), _message(1, YM, 0, 2), _message(0, ZP, 3, 0), _message(0, ZM, 2, 0)),
    (_message(1, YP, 0, 2), _message(1, YM, 1, 1), _message(0, ZP, 2, 0), _message(0, ZM, 1, 1)),
    (_message(1, YP, 3, 0), _message(1, YM, 1, 3), _message(0, ZP, 0, 3), _message(0, ZM, 3, 1)),
    (_message(1, YP, 3, 2), _message(0, ZP, 2, 3)),
)
NUMBER = {}
for _round in ROUNDS:
    for _m in _round:
        NUMBER[_m] = len(NUMBER)
MESSAGES = len(NUMBER)
SENT_FROM = {}
for _m in NUMBER:
    SENT_FROM.setdefault((_m[0], _m[2]), []).append(_m)

FEAT, COT, BIAS, PART, AGG, GRAD, OUT, WEIGHT, FINAL, END = 0, 2, 5, 8, 9, 10, 11, 12, 20, 22


def kernel(
    table,
    chain,
    feat,
    cot,
    weight,
    bias,
    edge,
    out_ref,
    gin_ref,
    gw_ref,
    gb_ref,
    blocks,
    blocks_t,
    gathered,
    acc,
    packed,
    swapped,
    cot_packed,
    cot_got,
    cot_full,
    bias_got,
    part_got,
    agg,
    pre_grad,
    grad_agg,
    out_half,
    wterm,
    wcore,
    wlink,
    wy,
    wz,
    shares,
    shares_got,
    final,
    final_got,
    edge_sem,
    send_sem,
    gather_sem,
    scatter_sem,
    odd_send,
    odd_recv,
):
    row, col = lax.axis_index("row"), lax.axis_index("col")
    y, a, z = row // 8, (row // 4) % 2, row % 4
    hi, b = col // 2, col % 2
    nslot = 16

    def device(yy, aa, zz, hh, bb):
        return ((yy * 2 + aa) * 4 + zz, hh * 2 + bb)

    def step(way):
        return device((y + way[0] + 4) % 4, a, (z + way[1] + 4) % 4, hi, b)

    def panel_of(slot):
        return (((y + slot // 4) % 4) * 2 + b) * 4 + (z + slot % 4) % 4

    loads = [
        pltpu.make_async_copy(
            edge.at[panel_of(s)], blocks.at[s, pl.ds(0, nslot)], edge_sem.at[s]
        )
        for s in range(nslot)
    ]
    for load in loads:
        load.start()

    partners = [device(y, 1 - a, z, hi, b), device(y, a, z, hi, 1 - b), device(y, 1 - a, z, hi, 1 - b)]
    partners += [device(y, a, z, 1 - hi, 0), device(y, a, z, 1 - hi, 1)]
    partners += [device((y + k) % 4, a, z, hi, b) for k in (1, 2, 3)]
    partners += [device(y, a, (z + k) % 4, hi, b) for k in (1, 2, 3)]
    barrier = pltpu.get_barrier_semaphore()
    for partner in partners:
        pl.semaphore_signal(barrier, inc=1, device_id=partner, device_id_type=MESH)

    packed[...] = jnp.concatenate([feat[:512, :], feat[512:, :]], axis=1)
    for half in range(2):
        cot_packed[half] = jnp.concatenate(
            [cot[half * 512 : half * 512 + 256, :], cot[half * 512 + 256 : half * 512 + 512, :]], axis=1
        )
    bias_row = bias[...]
    bias_got[col] = jnp.broadcast_to(jnp.concatenate([bias_row, bias_row], axis=1), (8, 128))
    pl.semaphore_wait(barrier, len(partners))

    def feature_copy(chip, core_from, target):
        return pltpu.make_async_remote_copy(
            src_ref=packed,
            dst_ref=swapped.at[core_from],
            send_sem=odd_send.at[FEAT + chip],
            recv_sem=odd_recv.at[FEAT + core_from],
            device_id=target,
            device_id_type=MESH,
        )

    for chip in range(2):
        here = jnp.logical_and(a == chip, a == b)

        @pl.when(jnp.logical_not(here))
        def _():
            feature_copy(chip, b, device(y, chip, z, hi, a)).start()

        @pl.when(here)
        def _():
            swapped[b] = packed[...]

    def cot_copy(k):
        other = (col + k) % 4
        return pltpu.make_async_remote_copy(
            src_ref=cot_packed.at[other % 2],
            dst_ref=cot_got.at[col],
            send_sem=odd_send.at[COT + k - 1],
            recv_sem=odd_recv.at[COT + k - 1],
            device_id=(row, other),
            device_id_type=MESH,
        )

    def cot_landed(k):
        return pltpu.make_async_remote_copy(
            src_ref=cot_packed.at[0],
            dst_ref=cot_got.at[(col + 4 - k) % 4],
            send_sem=odd_send.at[COT + k - 1],
            recv_sem=odd_recv.at[COT + k - 1],
            device_id=(row, (col + k) % 4),
            device_id_type=MESH,
        )

    def bias_copy(k, place):
        return pltpu.make_async_remote_copy(
            src_ref=bias_got.at[col],
            dst_ref=bias_got.at[place],
            send_sem=odd_send.at[BIAS + k - 1],
            recv_sem=odd_recv.at[BIAS + k - 1],
            device_id=(row, (col + k) % 4),
            device_id_type=MESH,
        )

    def merge(s):
        j = panel_of(s)
        blocks[s, nslot] = jnp.zeros((128, 128), BF)
        blocks_t[s, nslot] = jnp.zeros((128, 128), BF)

        def one(k, _):
            total = blocks[s, k] + blocks[s, chain[j * nslot + k]]
            blocks[s, k] = total
            blocks_t[s, k] = total.T
            return 0

        lax.fori_loop(0, nslot, one, 0)

    acc[...] = jnp.zeros_like(acc)
    for load in loads:
        load.wait()
    for s in range(nslot):
        merge(s)

    for core in range(2):

        @pl.when(jnp.logical_not(jnp.logical_and(a == b, core == b)))
        def _():
            feature_copy(0, core, device(y, 1 - a, z, hi, b)).wait_recv()

    first, second = swapped[0], swapped[1]
    gathered[0, 0] = jnp.concatenate([first[:, :64], second[:, :64]], axis=1)
    gathered[1, 0] = jnp.concatenate([first[:, 64:], second[:, 64:]], axis=1)

    def gather_copy(m):
        half, way, start, end = m
        return pltpu.make_async_remote_copy(
            src_ref=gathered.at[half, start],
            dst_ref=gathered.at[half, end],
            send_sem=send_sem.at[NUMBER[m]],
            recv_sem=gather_sem.at[NUMBER[m]],
            device_id=step(way),
            device_id_type=MESH,
        )

    def forward_unit(half, slot):
        j = panel_of(slot)

        def one(d, _):
            at = j * 64 + d * 8 + 4 * half
            lhs = jnp.concatenate([blocks[slot, table[at + s]] for s in range(4)], axis=1)
            acc[pl.ds(d * 128, 128), :] += jnp.dot(
                lhs, gathered[half, slot], preferred_element_type=F32
            )
            return 0

        lax.fori_loop(0, 8, one, 0)

    for m in ROUNDS[0] + ROUNDS[1]:
        gather_copy(m).start()
    for k in (1, 2, 3):
        cot_copy(k).start()
        bias_copy(k, col).start()
    cot_got[col] = cot_packed[b]
    forward_unit(0, 0)
    forward_unit(1, 0)
    for k, now in enumerate(ROUNDS):
        for m in now:
            gather_copy(m).wait_recv()
        if k + 2 < len(ROUNDS):
            for m in ROUNDS[k + 2]:
                gather_copy(m).start()
        for m in now:
            forward_unit(m[0], m[3])
        if k == 4:
            for other in (1, 2, 3):
                cot_landed(other).wait_recv()
                bias_copy(other, (col + 4 - other) % 4).wait_recv()
            cot_full[:256, :] = jnp.concatenate([cot_got[c][:, :64] for c in range(4)], axis=1)
            cot_full[256:, :] = jnp.concatenate([cot_got[c][:, 64:] for c in range(4)], axis=1)

    mine = pl.multiple_of(b * 512, 512)
    theirs = pl.multiple_of(512 - b * 512, 512)
    sibling = device(y, a, z, hi, 1 - b)
    part_copy = pltpu.make_async_remote_copy(
        src_ref=acc.at[pl.ds(theirs, 512)],
        dst_ref=part_got,
        send_sem=odd_send.at[PART],
        recv_sem=odd_recv.at[PART],
        device_id=sibling,
        device_id_type=MESH,
    )
    part_copy.start()
    for m in NUMBER:
        gather_copy(m).wait_send()
    part_copy.wait_recv()
    agg[hi] = (acc[pl.ds(mine, 512), :] + part_got[...]).astype(BF)
    agg_copy = pltpu.make_async_remote_copy(
        src_ref=agg.at[hi],
        dst_ref=agg.at[hi],
        send_sem=odd_send.at[AGG],
        recv_sem=odd_recv.at[AGG],
        device_id=device(y, a, z, 1 - hi, b),
        device_id_type=MESH,
    )
    agg_copy.start()
    agg_landed = pltpu.make_async_remote_copy(
        src_ref=agg.at[hi],
        dst_ref=agg.at[1 - hi],
        send_sem=odd_send.at[AGG],
        recv_sem=odd_recv.at[AGG],
        device_id=device(y, a, z, 1 - hi, b),
        device_id_type=MESH,
    )
    bias_all = jnp.concatenate([bias_got[c][0:1, :64] for c in range(4)], axis=1)
    agg_landed.wait_recv()

    def dense(t, bias_sum):
        at = pl.ds(pl.multiple_of(t * 128, 128), 128)
        pre = jnp.dot(agg[0, at, :], weight[:128, :], preferred_element_type=F32)
        pre += jnp.dot(agg[1, at, :], weight[128:, :], preferred_element_type=F32)
        pre += bias_all
        sig = jax.nn.sigmoid(pre)
        value = pre * sig
        out_half[b, at, :] = jnp.where(hi == 0, value[:, :128], value[:, 128:]).astype(BF)
        grad = (cot_full[at, :].astype(F32) * sig * (1.0 + pre * (1.0 - sig))).astype(BF)
        pre_grad[at, :] = grad
        grad_agg[b, at, :] = lax.dot_general(
            grad,
            weight[pl.ds(pl.multiple_of(hi * 128, 128), 128), :],
            (((1,), (1,)), ((), ())),
            preferred_element_type=F32,
        ).astype(BF)
        return bias_sum + jnp.sum(grad.astype(F32), axis=0, keepdims=True)

    bias_sum = lax.fori_loop(0, 4, dense, jnp.zeros((1, 256), F32))

    def pair_copy(ref, place, n):
        return pltpu.make_async_remote_copy(
            src_ref=ref.at[b],
            dst_ref=ref.at[place],
            send_sem=odd_send.at[n],
            recv_sem=odd_recv.at[n],
            device_id=sibling,
            device_id_type=MESH,
        )

    pair_copy(grad_agg, b, GRAD).start()
    pair_copy(out_half, b, OUT).start()

    term = lax.dot_general(
        agg[hi], pre_grad[...], (((0,), (0,)), ((), ())), preferred_element_type=F32
    )
    for core in range(2):
        wterm[core, :64] = term[core * 64 : core * 64 + 64, :]
        wterm[core, 64:] = jnp.broadcast_to(bias_sum, (8, 256))

    def weight_copy(src, dst, target, n):
        return pltpu.make_async_remote_copy(
            src_ref=src,
            dst_ref=dst,
            send_sem=odd_send.at[WEIGHT + n],
            recv_sem=odd_recv.at[WEIGHT + n],
            device_id=target,
            device_id_type=MESH,
        )

    weight_core = weight_copy(wterm.at[1 - b], wcore, sibling, 0)
    weight_core.start()
    weight_link = weight_copy(wlink.at[0], wlink.at[1], device(y, 1 - a, z, hi, b), 1)

    def weight_y(k, place):
        return weight_copy(wy.at[y], wy.at[place], device((y + k) % 4, a, z, hi, b), 1 + k)

    def weight_z(k, place):
        return weight_copy(wz.at[z], wz.at[place], device(y, a, (z + k) % 4, hi, b), 4 + k)

    def scatter_copy(m):
        half, way, start, end = m
        return pltpu.make_async_remote_copy(
            src_ref=shares.at[half, end],
            dst_ref=shares_got.at[NUMBER[m]],
            send_sem=send_sem.at[NUMBER[m]],
            recv_sem=scatter_sem.at[NUMBER[m]],
            device_id=step((-way[0], -way[1])),
            device_id_type=MESH,
        )

    def backward_unit(half, slot, keep):
        j = panel_of(slot)
        came = SENT_FROM.get((half, slot), ())
        for m in came:
            scatter_copy(m).wait_recv()

        def one(s, _):
            at = j * 64 + 4 * half + s
            total = jnp.zeros((128, 128), F32)
            for h in range(2):
                lhs = jnp.concatenate(
                    [blocks_t[slot, table[at + 8 * (4 * h + d)]] for d in range(4)], axis=1
                )
                total += jnp.dot(lhs, grad_agg[h], preferred_element_type=F32)
            rows = pl.ds(pl.multiple_of(s * 128, 128), 128)
            for m in came:
                total += shares_got[NUMBER[m], rows, :].astype(F32)
            keep(rows, total)
            return 0

        lax.fori_loop(0, 4, one, 0)

    pair_copy(grad_agg, 1 - b, GRAD).wait_recv()
    for k in range(len(ROUNDS) - 1, -1, -1):
        for m in ROUNDS[k]:
            half, end = m[0], m[3]

            def keep(rows, total):
                shares[half, end, rows, :] = total.astype(BF)

            backward_unit(half, end, keep)
            scatter_copy(m).start()
        if k == 7:
            weight_core.wait_recv()
            wlink[0] = wterm[b] + wcore[...]
            weight_link.start()
        if k == 5:
            weight_link.wait_recv()
            wy[y] = wlink[0] + wlink[1]
            for n in (1, 2, 3):
                weight_y(n, y).start()
        if k == 2:
            for n in (1, 2, 3):
                weight_y(n, (y + 4 - n) % 4).wait_recv()
            wz[z] = (wy[0] + wy[1]) + (wy[2] + wy[3])
            for n in (1, 2, 3):
                weight_z(n, z).start()

    pair_copy(out_half, 1 - b, OUT).wait_recv()
    for half in range(2):
        both = out_half[half]
        out_ref[half * 512 : half * 512 + 512, :] = jnp.where(b == 0, both[:, :64], both[:, 64:])

    for half in range(2):

        def keep_final(rows, total):
            shares[half, 0, rows, :] = total.astype(BF)

        backward_unit(half, 0, keep_final)
    low, high = shares[0, 0], shares[1, 0]
    final[0] = jnp.concatenate([low[:, :64], high[:, :64]], axis=1)
    final[1] = jnp.concatenate([low[:, 64:], high[:, 64:]], axis=1)

    def final_copy(core, chip_from, target):
        return pltpu.make_async_remote_copy(
            src_ref=final.at[core],
            dst_ref=final_got.at[chip_from],
            send_sem=odd_send.at[FINAL + core],
            recv_sem=odd_recv.at[FINAL + chip_from],
            device_id=target,
            device_id_type=MESH,
        )

    for core in range(2):
        here = jnp.logical_and(a == b, b == core)

        @pl.when(jnp.logical_not(here))
        def _():
            final_copy(core, a, device(y, b, z, hi, core)).start()

        @pl.when(here)
        def _():
            final_got[a] = final[core]

    for n in (1, 2, 3):
        weight_z(n, (z + 4 - n) % 4).wait_recv()
    scale = 1.0 / (32 * 1024) ** 0.5
    whole = ((wz[0] + wz[1]) + (wz[2] + wz[3])) * scale
    gw_ref[...] = whole[:64, :]
    gb = whole[64:65, :]
    own = jnp.where(hi == 0, gb[:, :128], gb[:, 128:])
    gb_ref[...] = jnp.where(b == 0, own[:, :64], own[:, 64:])

    for chip in range(2):

        @pl.when(jnp.logical_not(jnp.logical_and(a == b, chip == a)))
        def _():
            final_copy(0, chip, device(y, 1 - a, z, hi, b)).wait_recv()

    total = (final_got[0].astype(F32) + final_got[1].astype(F32)).astype(BF)
    gin_ref[:512, :] = total[:, :64]
    gin_ref[512:, :] = total[:, 64:]

    for chip in range(2):

        @pl.when(jnp.logical_not(jnp.logical_and(a == chip, a == b)))
        def _():
            feature_copy(chip, b, device(y, chip, z, hi, a)).wait_send()

    for k in (1, 2, 3):
        cot_copy(k).wait_send()
        bias_copy(k, col).wait_send()
        weight_y(k, y).wait_send()
        weight_z(k, z).wait_send()
    part_copy.wait_send()
    agg_copy.wait_send()
    pair_copy(grad_agg, b, GRAD).wait_send()
    pair_copy(out_half, b, OUT).wait_send()
    weight_core.wait_send()
    weight_link.wait_send()
    for m in NUMBER:
        scatter_copy(m).wait_send()
    for core in range(2):

        @pl.when(jnp.logical_not(jnp.logical_and(a == b, b == core)))
        def _():
            final_copy(core, a, device(y, b, z, hi, core)).wait_send()


def slot_tables(block_dst, block_src, counts):
    slots = block_dst.shape[1]
    k = jnp.arange(slots, dtype=jnp.int32)
    live = k[None, :] < counts[:, None]
    cell = jnp.where(live, block_dst * 8 + block_src, -1)
    places = jnp.arange(64, dtype=jnp.int32)
    hit = cell[:, None, :] == places[None, :, None]
    table = jnp.max(jnp.where(hit, k[None, None, :], -1), axis=2)
    table = jnp.where(table < 0, slots, table)
    before = (cell[:, None, :] == cell[:, :, None]) & (k[None, None, :] < k[None, :, None])
    chain = jnp.max(jnp.where(before & live[:, :, None], k[None, None, :], -1), axis=2)
    chain = jnp.where(chain < 0, slots, chain)
    return table.reshape(-1), chain.reshape(-1)


def body(features, weight, bias, edge_blocks, block_dst, block_src, counts, cotangent):
    table, chain = slot_tables(block_dst[0], block_src[0], counts[0])
    vmem = pl.BlockSpec(memory_space=pltpu.VMEM)
    smem = pl.BlockSpec(memory_space=pltpu.SMEM)
    out, gin, gw, gb = pl.pallas_call(
        kernel,
        out_shape=(
            jax.ShapeDtypeStruct((1024, 64), BF),
            jax.ShapeDtypeStruct((1024, 64), BF),
            jax.ShapeDtypeStruct((64, 256), F32),
            jax.ShapeDtypeStruct((1, 64), F32),
        ),
        in_specs=[smem, smem, vmem, vmem, vmem, vmem, pl.BlockSpec(memory_space=pl.ANY)],
        out_specs=(vmem, vmem, vmem, vmem),
        scratch_shapes=[
            pltpu.VMEM((16, 17, 128, 128), BF),
            pltpu.VMEM((16, 17, 128, 128), BF),
            pltpu.VMEM((2, 16, 512, 128), BF),
            pltpu.VMEM((1024, 128), F32),
            pltpu.VMEM((512, 128), BF),
            pltpu.VMEM((2, 512, 128), BF),
            pltpu.VMEM((2, 256, 128), BF),
            pltpu.VMEM((4, 256, 128), BF),
            pltpu.VMEM((512, 256), BF),
            pltpu.VMEM((4, 8, 128), F32),
            pltpu.VMEM((512, 128), F32),
            pltpu.VMEM((2, 512, 128), BF),
            pltpu.VMEM((512, 256), BF),
            pltpu.VMEM((2, 512, 128), BF),
            pltpu.VMEM((2, 512, 128), BF),
            pltpu.VMEM((2, 72, 256), F32),
            pltpu.VMEM((72, 256), F32),
            pltpu.VMEM((2, 72, 256), F32),
            pltpu.VMEM((4, 72, 256), F32),
            pltpu.VMEM((4, 72, 256), F32),
            pltpu.VMEM((2, 16, 512, 128), BF),
            pltpu.VMEM((MESSAGES, 512, 128), BF),
            pltpu.VMEM((2, 512, 128), BF),
            pltpu.VMEM((2, 512, 128), BF),
            pltpu.SemaphoreType.DMA((16,)),
            pltpu.SemaphoreType.DMA((MESSAGES,)),
            pltpu.SemaphoreType.DMA((MESSAGES,)),
            pltpu.SemaphoreType.DMA((MESSAGES,)),
            pltpu.SemaphoreType.DMA((END,)),
            pltpu.SemaphoreType.DMA((END,)),
        ],
        compiler_params=pltpu.CompilerParams(
            collective_id=0, has_side_effects=True, vmem_limit_bytes=56 * 1024 * 1024
        ),
        name="graph_layer",
    )(table, chain, features, cotangent, weight, bias.reshape(1, 64), edge_blocks[0])
    return out, gin, gw, gb.reshape(64)


def solution(mesh):
    return jax.shard_map(
        body,
        mesh=mesh,
        in_specs=(
            P("row", "col"),
            P(),
            P("col"),
            P("row", None, None, None, None),
            P("row", None, None),
            P("row", None, None),
            P("row", None),
            P("row", "col"),
        ),
        out_specs=(P("row", "col"), P("row", "col"), P("col", None), P("col")),
        check_vma=False,
    )
```

```python
import functools

import jax
import jax.numpy as jnp
from jax import lax
from jax.experimental import pallas as pl
from jax.experimental.pallas import tpu as pltpu
from jax.sharding import PartitionSpec as P

MESH = pl.DeviceIdType.MESH
BF = jnp.bfloat16
F32 = jnp.float32

YP, YM, ZP, ZM = (1, 0), (-1, 0), (0, 1), (0, -1)


def _message(half, way, dy, dz):
    return (half, way, 4 * dy + dz, 4 * ((dy - way[0]) % 4) + (dz - way[1]) % 4)


ROUNDS = (
    (_message(0, YP, 0, 0), _message(0, YM, 0, 0), _message(0, ZP, 0, 0), _message(0, ZM, 0, 0)),
    (_message(1, ZP, 0, 0), _message(1, ZM, 0, 0), _message(1, YP, 0, 0), _message(1, YM, 0, 0)),
    (_message(0, YP, 3, 0), _message(0, ZP, 1, 0), _message(0, ZM, 1, 0)),
    (_message(1, YP, 0, 1), _message(1, YM, 0, 1), _message(1, ZP, 0, 3), _message(0, ZM, 3, 0)),
    (_message(1, YP, 0, 3), _message(1, YM, 0, 3), _message(0, ZP, 3, 0), _message(0, ZM, 2, 0)),
    (_message(1, YP, 0, 2), _message(1, YM, 0, 2), _message(0, ZP, 2, 0), _message(0, ZM, 1, 1)),
    (_message(1, YP, 3, 0), _message(1, YM, 1, 1), _message(0, ZP, 0, 3), _message(0, ZM, 3, 1)),
    (_message(1, YP, 3, 2), _message(1, YM, 1, 3), _message(0, ZP, 2, 3)),
)
NUMBER = {}
for _round in ROUNDS:
    for _m in _round:
        NUMBER[_m] = len(NUMBER)
MESSAGES = len(NUMBER)
SENT_FROM = {}
for _m in NUMBER:
    SENT_FROM.setdefault((_m[0], _m[2]), []).append(_m)

FEAT, COT, BIAS, PART, AGG, GRAD, OUT, WEIGHT, FINAL, END = 0, 4, 7, 10, 14, 18, 22, 23, 31, 35
CONTRACT_LAST = (((1,), (1,)), ((), ()))


def choose(i, values):
    chosen = jnp.int32(values[0])
    for n, value in enumerate(values[1:], 1):
        chosen = jnp.where(i == n, jnp.int32(value), chosen)
    return chosen


def kernel(
    dst_ids,
    src_ids,
    counts,
    feat,
    cot,
    weight,
    bias,
    edge,
    out_ref,
    gin_ref,
    gw_ref,
    gb_ref,
    blocks,
    gathered,
    acc,
    cot_all,
    bias_got,
    bias_col,
    weight_t,
    part_got,
    agg,
    pre_grad,
    grad_agg,
    out_half,
    out_got,
    wterm,
    wcore,
    wlink,
    wy,
    wz,
    part,
    own_part,
    shares,
    shares_got,
    final,
    final_got,
    lists,
    slots,
    list_sem,
    edge_sem,
    send_sem,
    gather_sem,
    scatter_sem,
    odd_send,
    odd_recv,
):
    row, col = lax.axis_index("row"), lax.axis_index("col")
    y, a, z = row // 8, (row // 4) % 2, row % 4
    hi, b = col // 2, col % 2
    nslot = 16

    def device(yy, aa, zz, hh, bb):
        return ((yy * 2 + aa) * 4 + zz, hh * 2 + bb)

    def step(way):
        return device((y + way[0] + 4) % 4, a, (z + way[1] + 4) % 4, hi, b)

    def panel_of(slot):
        return (((y + slot // 4) % 4) * 2 + b) * 4 + (z + slot % 4) % 4

    def rows64(core):
        return pl.ds(pl.multiple_of(core * 64, 64), 64)

    def remote(src, dst, n_send, n_recv, target):
        return pltpu.make_async_remote_copy(
            src_ref=src,
            dst_ref=dst,
            send_sem=odd_send.at[n_send],
            recv_sem=odd_recv.at[n_recv],
            device_id=target,
            device_id_type=MESH,
        )

    partners = [device(y, 1 - a, z, hi, b), device(y, a, z, hi, 1 - b), device(y, 1 - a, z, hi, 1 - b)]
    partners += [device(y, a, z, 1 - hi, 0), device(y, a, z, 1 - hi, 1)]
    partners += [device((y + k) % 4, a, z, hi, b) for k in (1, 2, 3)]
    partners += [device(y, a, (z + k) % 4, hi, b) for k in (1, 2, 3)]
    barrier = pltpu.get_barrier_semaphore()
    for partner in partners:
        pl.semaphore_signal(barrier, inc=1, device_id=partner, device_id_type=MESH)

    loads = [
        pltpu.make_async_copy(
            edge.at[panel_of(s)], blocks.at[s, pl.ds(0, nslot)], edge_sem.at[s]
        )
        for s in range(nslot)
    ]
    for load in loads:
        load.start()

    k_of = lax.broadcasted_iota(jnp.int32, (nslot, 32), 0)
    cell = jnp.where(k_of < counts[...], dst_ids[...] * 8 + src_ids[...], -1)
    place = lax.broadcasted_iota(jnp.int32, (64, 32), 0)
    found = jnp.full((64, 32), nslot, jnp.int32)
    before = jnp.full((nslot, 32), nslot, jnp.int32)
    for k in range(nslot):
        before = jnp.where((cell == cell[k : k + 1, :]) & (k_of > k) & (cell >= 0), k, before)
        found = jnp.where(place == cell[k : k + 1, :], k, found)
    lists[...] = jnp.zeros_like(lists)
    lists[:64, :32] = found
    lists[64:, :32] = before
    list_copy = pltpu.make_async_copy(lists, slots, list_sem)
    list_copy.start()

    bias_row = bias[...]
    bias_got[col] = jnp.broadcast_to(jnp.concatenate([bias_row, bias_row], axis=1), (8, 128))
    pl.semaphore_wait(barrier, len(partners))

    def feature_copy(half, chip, core_from, target):
        return remote(
            feat.at[:, pl.ds(half * 512, 512)],
            gathered.at[half, 0, rows64(core_from)],
            FEAT + 2 * half + chip,
            FEAT + 2 * half + core_from,
            target,
        )

    for half in range(2):
        for chip in range(2):
            here = jnp.logical_and(a == chip, a == b)

            @pl.when(jnp.logical_not(here))
            def _():
                feature_copy(half, chip, b, device(y, chip, z, hi, a)).start()

            @pl.when(here)
            def _():
                gathered[half, 0, rows64(b), :] = feat[:, half * 512 : half * 512 + 512]

    def feature_landed(half):
        for core in range(2):

            @pl.when(jnp.logical_not(jnp.logical_and(a == b, core == b)))
            def _():
                feature_copy(half, 0, core, device(y, 1 - a, z, hi, b)).wait_recv()

    def gather_copy(m):
        half, way, start, end = m
        return pltpu.make_async_remote_copy(
            src_ref=gathered.at[half, start],
            dst_ref=gathered.at[half, end],
            send_sem=send_sem.at[NUMBER[m]],
            recv_sem=gather_sem.at[NUMBER[m]],
            device_id=step(way),
            device_id_type=MESH,
        )

    def cot_copy(k):
        other = (col + k) % 4
        return remote(
            cot.at[:, pl.ds(pl.multiple_of((other % 2) * 512, 512), 512)],
            cot_all.at[rows64(col)],
            COT + k - 1,
            COT + k - 1,
            (row, other),
        )

    def cot_landed(k):
        return remote(
            cot.at[:, pl.ds(0, 512)],
            cot_all.at[rows64((col + 4 - k) % 4)],
            COT + k - 1,
            COT + k - 1,
            (row, (col + k) % 4),
        )

    def bias_copy(k, place):
        return remote(bias_got.at[col], bias_got.at[place], BIAS + k - 1, BIAS + k - 1, (row, (col + k) % 4))

    for half in range(2):
        feature_landed(half)
        for m in ROUNDS[half]:
            gather_copy(m).start()
    for k in (1, 2, 3):
        cot_copy(k).start()
        bias_copy(k, col).start()
    cot_all[rows64(col), :] = cot[:, pl.ds(pl.multiple_of(b * 512, 512), 512)]

    acc[...] = jnp.zeros_like(acc)
    weight_t[...] = weight[...].T
    list_copy.wait()
    for load in loads:
        load.wait()

    def merge(s, _):
        j = panel_of(s)
        blocks[s, nslot] = jnp.zeros((128, 128), BF)
        for k in range(1, nslot):
            blocks[s, k] = blocks[s, k] + blocks[s, slots[64 + k, j]]
        return 0

    lax.fori_loop(0, nslot, merge, 0)

    def forward_units(units):
        def one(i, _):
            half = choose(i, [u[0] for u in units])
            slot = choose(i, [u[1] for u in units])
            j, at = panel_of(slot), 4 * half
            x = gathered[half, slot]
            for q in range(4):
                placed = jnp.concatenate(
                    [
                        jnp.concatenate([blocks[slot, slots[at + 8 * d + s, j]] for s in range(4)], axis=1)
                        for d in (2 * q, 2 * q + 1)
                    ],
                    axis=0,
                )
                acc[:, 256 * q : 256 * q + 256] += lax.dot_general(
                    x, placed, CONTRACT_LAST, preferred_element_type=F32
                )
            return 0

        lax.fori_loop(0, len(units), one, 0)

    forward_units(((0, 0), (1, 0)))
    for k, now in enumerate(ROUNDS):
        for m in now:
            gather_copy(m).wait_recv()
        if k + 2 < len(ROUNDS):
            for m in ROUNDS[k + 2]:
                gather_copy(m).start()
        forward_units([(m[0], m[3]) for m in now])
        if k == 4:
            for other in (1, 2, 3):
                cot_landed(other).wait_recv()
                bias_copy(other, (col + 4 - other) % 4).wait_recv()
            for h in range(2):
                lanes = jnp.concatenate([bias_got[2 * h][0:1, :64], bias_got[2 * h + 1][0:1, :64]], axis=1)
                bias_col[h * 128 : h * 128 + 128, :] = jnp.broadcast_to(lanes, (128, 128)).T

    sibling = device(y, a, z, hi, 1 - b)
    peer = device(y, a, z, 1 - hi, b)
    own_rows = pl.ds(pl.multiple_of(hi * 128, 128), 128)
    peer_rows = pl.ds(pl.multiple_of(128 - hi * 128, 128), 128)

    def lanes(t):
        return pl.ds(t * 128, 128)

    def part_copy(t):
        theirs = pl.ds(pl.multiple_of((1 - b) * 512 + t * 128, 128), 128)
        return remote(acc.at[:, theirs], part_got.at[t], PART + t, PART + t, sibling)

    def agg_copy(t, rows):
        return remote(agg.at[own_rows, lanes(t)], agg.at[rows, lanes(t)], AGG + t, AGG + t, peer)

    def grad_copy(t, core):
        return remote(grad_agg.at[4 * b + t], grad_agg.at[4 * core + t], GRAD + t, GRAD + t, sibling)

    for t in range(4):
        part_copy(t).start()
    for t in range(4):
        part_copy(t).wait_recv()
        mine = pl.ds(pl.multiple_of(b * 512 + t * 128, 128), 128)
        agg[own_rows, lanes(t)] = (acc[:, mine] + part_got[t]).astype(BF)
        agg_copy(t, own_rows).start()
    for m in NUMBER:
        gather_copy(m).wait_send()
    for t in range(4):
        agg_copy(t, peer_rows).wait_recv()
        pre = jnp.dot(weight_t[...], agg[:, lanes(t)], preferred_element_type=F32) + bias_col[...]
        sig = jax.nn.sigmoid(pre)
        value = pre * sig
        grad = (cot_all[:, lanes(t)].astype(F32) * sig * (1.0 + pre * (1.0 - sig))).astype(BF)
        pre_grad[:, lanes(t)] = grad
        grad_agg[4 * b + t] = jnp.dot(weight[own_rows, :], grad, preferred_element_type=F32).astype(BF)
        grad_copy(t, b).start()
        out_half[:, lanes(t)] = jnp.where(hi == 0, value[:128], value[128:]).astype(BF)
    out_copy = remote(out_half.at[rows64(1 - b)], out_got, OUT, OUT, sibling)
    out_copy.start()

    term = lax.dot_general(agg[own_rows, :], pre_grad[...], CONTRACT_LAST, preferred_element_type=F32)
    bias_term = lax.dot_general(jnp.ones((16, 512), BF), pre_grad[...], CONTRACT_LAST, preferred_element_type=F32)
    for core in range(2):
        wterm[core, :64] = term[core * 64 : core * 64 + 64, :]
        wterm[core, 64:] = bias_term
    weight_core = remote(wterm.at[1 - b], wcore, WEIGHT, WEIGHT, sibling)
    weight_core.start()
    weight_link = remote(wlink.at[0], wlink.at[1], WEIGHT + 1, WEIGHT + 1, device(y, 1 - a, z, hi, b))

    def weight_y(k, place):
        return remote(
            wy.at[y], wy.at[place], WEIGHT + 1 + k, WEIGHT + 1 + k, device((y + k) % 4, a, z, hi, b)
        )

    def weight_z(k, place):
        return remote(
            wz.at[z], wz.at[place], WEIGHT + 4 + k, WEIGHT + 4 + k, device(y, a, (z + k) % 4, hi, b)
        )

    def scatter_copy(m):
        half, way, start, end = m
        return pltpu.make_async_remote_copy(
            src_ref=shares.at[half, end],
            dst_ref=shares_got.at[NUMBER[m]],
            send_sem=send_sem.at[NUMBER[m]],
            recv_sem=scatter_sem.at[NUMBER[m]],
            device_id=step((-way[0], -way[1])),
            device_id_type=MESH,
        )

    def backward_units(units, result):
        def one(i, _):
            half = choose(i, [u[0] for u in units])
            slot = choose(i, [u[1] for u in units])
            j, at = panel_of(slot), 4 * half
            grads = jnp.concatenate([grad_agg[d] for d in range(8)], axis=1)
            for s in (0, 2):
                placed = jnp.concatenate(
                    [
                        jnp.concatenate([blocks[slot, slots[at + 8 * d + s + e, j]] for e in (0, 1)], axis=1)
                        for d in range(8)
                    ],
                    axis=0,
                )
                result[i, :, s * 128 : s * 128 + 256] = jnp.dot(
                    grads, placed, preferred_element_type=F32
                )
            return 0

        lax.fori_loop(0, len(units), one, 0)

    def with_arrivals(half, slot, result, i):
        total = result[i]
        for m in SENT_FROM.get((half, slot), ()):
            scatter_copy(m).wait_recv()
            total = total + shares_got[NUMBER[m]].astype(F32)
        return total.astype(BF)

    for t in range(4):
        grad_copy(t, 1 - b).wait_recv()
    for k in range(len(ROUNDS) - 1, -1, -1):
        now = ROUNDS[k]
        backward_units([(m[0], m[3]) for m in now], part)
        for i, m in enumerate(now):
            shares[m[0], m[3]] = with_arrivals(m[0], m[3], part, i)
            scatter_copy(m).start()
        if k == 7:
            weight_core.wait_recv()
            wlink[0] = wterm[b] + wcore[...]
            weight_link.start()
        if k == 5:
            weight_link.wait_recv()
            wy[y] = (wlink[0] + wlink[1]).astype(BF)
            for n in (1, 2, 3):
                weight_y(n, y).start()
        if k == 2:
            for n in (1, 2, 3):
                weight_y(n, (y + 4 - n) % 4).wait_recv()
            wz[z] = sum(wy[n].astype(F32) for n in range(4)).astype(BF)
            for n in (1, 2, 3):
                weight_z(n, z).start()

    backward_units(((0, 0), (1, 0)), own_part)
    out_copy.wait_recv()
    for half in range(2):
        at = slice(half * 512, half * 512 + 512)
        out_ref[:, at] = jnp.where(b == half, out_half[rows64(b), :], out_got[...])

    def final_copy(half, core, chip_from, target):
        lane = pl.ds(half * 512, 512)
        return remote(
            final.at[half, pl.ds(core * 64, 64)],
            final_got.at[chip_from, :, lane],
            FINAL + 2 * half + core,
            FINAL + 2 * half + chip_from,
            target,
        )

    for half in (1, 0):
        final[half] = with_arrivals(half, 0, own_part, half)
        for core in range(2):
            here = jnp.logical_and(a == b, b == core)

            @pl.when(jnp.logical_not(here))
            def _():
                final_copy(half, core, a, device(y, b, z, hi, core)).start()

            @pl.when(here)
            def _():
                final_got[a, :, half * 512 : half * 512 + 512] = final[half, core * 64 : core * 64 + 64, :]

    for n in (1, 2, 3):
        weight_z(n, (z + 4 - n) % 4).wait_recv()
    scale = 1.0 / (32 * 1024) ** 0.5
    whole = sum(wz[n].astype(F32) for n in range(4)) * scale
    gw_ref[...] = whole[:64, :]
    gb = whole[64:65, :]
    own = jnp.where(hi == 0, gb[:, :128], gb[:, 128:])
    gb_ref[...] = jnp.where(b == 0, own[:, :64], own[:, 64:])

    for half in (1, 0):
        for chip in range(2):

            @pl.when(jnp.logical_not(jnp.logical_and(a == b, chip == a)))
            def _():
                final_copy(half, 0, chip, device(y, 1 - a, z, hi, b)).wait_recv()

        at = slice(half * 512, half * 512 + 512)
        gin_ref[:, at] = (final_got[0, :, at].astype(F32) + final_got[1, :, at].astype(F32)).astype(BF)

    for half in range(2):
        for chip in range(2):

            @pl.when(jnp.logical_not(jnp.logical_and(a == chip, a == b)))
            def _():
                feature_copy(half, chip, b, device(y, chip, z, hi, a)).wait_send()

            @pl.when(jnp.logical_not(jnp.logical_and(a == b, b == chip)))
            def _():
                final_copy(half, chip, a, device(y, b, z, hi, chip)).wait_send()

    for k in (1, 2, 3):
        cot_copy(k).wait_send()
        bias_copy(k, col).wait_send()
        weight_y(k, y).wait_send()
        weight_z(k, z).wait_send()
    for t in range(4):
        part_copy(t).wait_send()
        agg_copy(t, own_rows).wait_send()
        grad_copy(t, b).wait_send()
    out_copy.wait_send()
    weight_core.wait_send()
    weight_link.wait_send()
    for m in NUMBER:
        scatter_copy(m).wait_send()


def hand_over(*refs):
    half = len(refs) // 2
    for n in range(half):
        refs[half + n][...] = refs[n][...]


def body(features, weight, bias, edge_blocks, block_dst, block_src, counts, cotangent):
    vmem = pl.BlockSpec(memory_space=pltpu.VMEM)
    out, gin, gw, gb = pl.pallas_call(
        kernel,
        out_shape=(
            jax.ShapeDtypeStruct((64, 1024), BF),
            jax.ShapeDtypeStruct((64, 1024), BF),
            jax.ShapeDtypeStruct((64, 256), F32),
            jax.ShapeDtypeStruct((1, 64), F32),
        ),
        in_specs=[vmem, vmem, vmem, vmem, vmem, vmem, vmem, pl.BlockSpec(memory_space=pl.ANY)],
        out_specs=(vmem, vmem, vmem, vmem),
        scratch_shapes=[
            pltpu.VMEM((16, 17, 128, 128), BF),
            pltpu.VMEM((2, 16, 128, 512), BF),
            pltpu.VMEM((128, 1024), F32),
            pltpu.VMEM((256, 512), BF),
            pltpu.VMEM((4, 8, 128), F32),
            pltpu.VMEM((256, 128), F32),
            pltpu.VMEM((256, 256), BF),
            pltpu.VMEM((4, 128, 128), F32),
            pltpu.VMEM((256, 512), BF),
            pltpu.VMEM((256, 512), BF),
            pltpu.VMEM((8, 128, 128), BF),
            pltpu.VMEM((128, 512), BF),
            pltpu.VMEM((64, 512), BF),
            pltpu.VMEM((2, 80, 256), F32),
            pltpu.VMEM((80, 256), F32),
            pltpu.VMEM((2, 80, 256), F32),
            pltpu.VMEM((4, 80, 256), BF),
            pltpu.VMEM((4, 80, 256), BF),
            pltpu.VMEM((4, 128, 512), F32),
            pltpu.VMEM((2, 128, 512), F32),
            pltpu.VMEM((2, 16, 128, 512), BF),
            pltpu.VMEM((MESSAGES, 128, 512), BF),
            pltpu.VMEM((2, 128, 512), BF),
            pltpu.VMEM((2, 64, 1024), BF),
            pltpu.VMEM((80, 128), jnp.int32),
            pltpu.SMEM((80, 128), jnp.int32),
            pltpu.SemaphoreType.DMA,
            pltpu.SemaphoreType.DMA((16,)),
            pltpu.SemaphoreType.DMA((MESSAGES,)),
            pltpu.SemaphoreType.DMA((MESSAGES,)),
            pltpu.SemaphoreType.DMA((MESSAGES,)),
            pltpu.SemaphoreType.DMA((END,)),
            pltpu.SemaphoreType.DMA((END,)),
        ],
        compiler_params=pltpu.CompilerParams(
            collective_id=0, has_side_effects=True, vmem_limit_bytes=56 * 1024 * 1024
        ),
        name="graph_layer",
    )(block_dst[0].T, block_src[0].T, counts, features.T, cotangent.T, weight, bias.reshape(1, 64), edge_blocks[0])
    results = (out, gin, gw, gb)
    out, gin, gw, gb = pl.pallas_call(
        hand_over,
        out_shape=tuple(jax.ShapeDtypeStruct(x.shape, x.dtype) for x in results),
        in_specs=[vmem] * 4,
        out_specs=(vmem,) * 4,
        name="hand_over",
    )(*results)
    return out.T, gin.T, gw, gb.reshape(64)


def solution(mesh):
    return jax.shard_map(
        body,
        mesh=mesh,
        in_specs=(
            P("row", "col"),
            P(),
            P("col"),
            P("row", None, None, None, None),
            P("row", None, None),
            P("row", None, None),
            P("row", None),
            P("row", "col"),
        ),
        out_specs=(P("row", "col"), P("row", "col"), P("col", None), P("col")),
        check_vma=False,
    )
```

```python
import functools

import jax
import jax.numpy as jnp
from jax import lax
from jax.experimental import pallas as pl
from jax.experimental.pallas import tpu as pltpu
from jax.sharding import PartitionSpec as P

MESH = pl.DeviceIdType.MESH
BF = jnp.bfloat16
F32 = jnp.float32

YP, YM, ZP, ZM = (1, 0), (-1, 0), (0, 1), (0, -1)


def _message(half, way, dy, dz):
    return (half, way, 4 * dy + dz, 4 * ((dy - way[0]) % 4) + (dz - way[1]) % 4)


ROUNDS = (
    (_message(0, YP, 0, 0), _message(0, YM, 0, 0), _message(0, ZP, 0, 0), _message(0, ZM, 0, 0)),
    (_message(1, ZP, 0, 0), _message(1, ZM, 0, 0), _message(1, YP, 0, 0), _message(1, YM, 0, 0)),
    (_message(0, YP, 3, 0), _message(0, ZP, 1, 0), _message(0, ZM, 1, 0)),
    (_message(1, YP, 0, 1), _message(1, YM, 0, 1), _message(1, ZP, 0, 3), _message(0, ZM, 3, 0)),
    (_message(1, YP, 0, 3), _message(1, YM, 0, 3), _message(0, ZP, 3, 0), _message(0, ZM, 2, 0)),
    (_message(1, YP, 0, 2), _message(1, YM, 0, 2), _message(0, ZP, 2, 0), _message(0, ZM, 1, 1)),
    (_message(1, YP, 3, 0), _message(1, YM, 1, 1), _message(0, ZP, 0, 3), _message(0, ZM, 3, 1)),
    (_message(1, YP, 3, 2), _message(1, YM, 1, 3), _message(0, ZP, 2, 3)),
)
NUMBER = {}
for _round in ROUNDS:
    for _m in _round:
        NUMBER[_m] = len(NUMBER)
MESSAGES = len(NUMBER)
PIECES = 2
ROWS = 128 // PIECES
SENT_FROM = {}
for _m in NUMBER:
    SENT_FROM.setdefault((_m[0], _m[2]), []).append(_m)

LEAVES = tuple(
    m
    for now in ROUNDS[:6]
    for m in now
    if (m[0], m[3]) not in SENT_FROM and m != _message(0, ZM, 1, 1)
)
FEAT, COT, BIAS, PART, AGG, GRAD, OUT, WEIGHT, FINAL, END = 0, 4, 7, 10, 14, 18, 22, 23, 31, 35
CONTRACT_LAST = (((1,), (1,)), ((), ()))


def choose(i, values):
    chosen = jnp.int32(values[0])
    for n, value in enumerate(values[1:], 1):
        chosen = jnp.where(i == n, jnp.int32(value), chosen)
    return chosen


def kernel(
    dst_ids,
    src_ids,
    counts,
    feat,
    cot,
    weight,
    bias,
    edge,
    out_ref,
    gin_ref,
    gw_ref,
    gb_ref,
    blocks,
    gathered,
    acc,
    cot_all,
    bias_got,
    bias_col,
    weight_t,
    part_got,
    agg,
    pre_grad,
    grad_agg,
    out_half,
    out_got,
    wterm,
    wcore,
    wlink,
    wy,
    wz,
    part,
    own_part,
    shares,
    shares_got,
    final,
    final_got,
    lists,
    slots,
    link_got,
    leaf_part,
    list_sem,
    link_send,
    link_recv,
    link_back,
    edge_sem,
    send_sem,
    gather_sem,
    scatter_sem,
    odd_send,
    odd_recv,
):
    row, col = lax.axis_index("row"), lax.axis_index("col")
    y, a, z = row // 8, (row // 4) % 2, row % 4
    hi, b = col // 2, col % 2
    nslot = 16
    diag = a == b
    off_diag = jnp.logical_not(diag)

    def unless_leaf(m, run):
        if m in LEAVES:
            pl.when(diag)(run)
        else:
            run()


    def device(yy, aa, zz, hh, bb):
        return ((yy * 2 + aa) * 4 + zz, hh * 2 + bb)

    def step(way):
        return device((y + way[0] + 4) % 4, a, (z + way[1] + 4) % 4, hi, b)

    def panel_of(slot):
        return (((y + slot // 4) % 4) * 2 + b) * 4 + (z + slot % 4) % 4

    def rows64(core):
        return pl.ds(pl.multiple_of(core * 64, 64), 64)

    def remote(src, dst, n_send, n_recv, target):
        return pltpu.make_async_remote_copy(
            src_ref=src,
            dst_ref=dst,
            send_sem=odd_send.at[n_send],
            recv_sem=odd_recv.at[n_recv],
            device_id=target,
            device_id_type=MESH,
        )

    partners = [device(y, 1 - a, z, hi, b), device(y, a, z, hi, 1 - b), device(y, 1 - a, z, hi, 1 - b)]
    partners += [device(y, a, z, 1 - hi, 0), device(y, a, z, 1 - hi, 1)]
    partners += [device((y + k) % 4, a, z, hi, b) for k in (1, 2, 3)]
    partners += [device(y, a, (z + k) % 4, hi, b) for k in (1, 2, 3)]
    barrier = pltpu.get_barrier_semaphore()
    for partner in partners:
        pl.semaphore_signal(barrier, inc=1, device_id=partner, device_id_type=MESH)

    loads = [
        pltpu.make_async_copy(
            edge.at[panel_of(s)], blocks.at[s, pl.ds(0, nslot)], edge_sem.at[s]
        )
        for s in range(nslot)
    ]
    for load in loads:
        load.start()

    k_of = lax.broadcasted_iota(jnp.int32, (nslot, 32), 0)
    cell = jnp.where(k_of < counts[...], dst_ids[...] * 8 + src_ids[...], -1)
    place = lax.broadcasted_iota(jnp.int32, (64, 32), 0)
    found = jnp.full((64, 32), nslot, jnp.int32)
    before = jnp.full((nslot, 32), nslot, jnp.int32)
    for k in range(nslot):
        before = jnp.where((cell == cell[k : k + 1, :]) & (k_of > k) & (cell >= 0), k, before)
        found = jnp.where(place == cell[k : k + 1, :], k, found)
    lists[...] = jnp.zeros_like(lists)
    lists[:64, :32] = found
    lists[64:, :32] = before
    list_copy = pltpu.make_async_copy(lists, slots, list_sem)
    list_copy.start()

    bias_row = bias[...]
    bias_got[col] = jnp.broadcast_to(jnp.concatenate([bias_row, bias_row], axis=1), (8, 128))
    pl.semaphore_wait(barrier, len(partners))

    def feature_copy(half, chip, core_from, target):
        return remote(
            feat.at[:, pl.ds(half * 512, 512)],
            gathered.at[half, 0, rows64(core_from)],
            FEAT + 2 * half + chip,
            FEAT + 2 * half + core_from,
            target,
        )

    for half in range(2):
        for chip in range(2):
            here = jnp.logical_and(a == chip, a == b)

            @pl.when(jnp.logical_not(here))
            def _():
                feature_copy(half, chip, b, device(y, chip, z, hi, a)).start()

            @pl.when(here)
            def _():
                gathered[half, 0, rows64(b), :] = feat[:, half * 512 : half * 512 + 512]

    def feature_landed(half):
        for core in range(2):

            @pl.when(jnp.logical_not(jnp.logical_and(a == b, core == b)))
            def _():
                feature_copy(half, 0, core, device(y, 1 - a, z, hi, b)).wait_recv()

    def gather_copy(m, piece):
        half, way, start, end = m
        n = PIECES * NUMBER[m] + piece
        rows = pl.ds(piece * ROWS, ROWS)
        return pltpu.make_async_remote_copy(
            src_ref=gathered.at[half, start, rows],
            dst_ref=gathered.at[half, end, rows],
            send_sem=send_sem.at[n],
            recv_sem=gather_sem.at[n],
            device_id=step(way),
            device_id_type=MESH,
        )

    def link_copy(m):
        n = LEAVES.index(m)
        return pltpu.make_async_remote_copy(
            src_ref=gathered.at[m[0], m[3]],
            dst_ref=gathered.at[m[0], m[3]],
            send_sem=link_send.at[n],
            recv_sem=link_recv.at[n],
            device_id=device(y, 1 - a, z, hi, b),
            device_id_type=MESH,
        )

    def cot_copy(k):
        other = (col + k) % 4
        return remote(
            cot.at[:, pl.ds(pl.multiple_of((other % 2) * 512, 512), 512)],
            cot_all.at[rows64(col)],
            COT + k - 1,
            COT + k - 1,
            (row, other),
        )

    def cot_landed(k):
        return remote(
            cot.at[:, pl.ds(0, 512)],
            cot_all.at[rows64((col + 4 - k) % 4)],
            COT + k - 1,
            COT + k - 1,
            (row, (col + k) % 4),
        )

    def bias_copy(k, place):
        return remote(bias_got.at[col], bias_got.at[place], BIAS + k - 1, BIAS + k - 1, (row, (col + k) % 4))

    for half in range(2):
        feature_landed(half)
        for piece in range(PIECES):
            for m in ROUNDS[half]:
                unless_leaf(m, lambda: gather_copy(m, piece).start())
    for k in (1, 2, 3):
        cot_copy(k).start()
        bias_copy(k, col).start()
    cot_all[rows64(col), :] = cot[:, pl.ds(pl.multiple_of(b * 512, 512), 512)]

    acc[...] = jnp.zeros_like(acc)
    weight_t[...] = weight[...].T
    list_copy.wait()
    for load in loads:
        load.wait()

    def merge(s, _):
        j = panel_of(s)
        blocks[s, nslot] = jnp.zeros((128, 128), BF)
        for k in range(1, nslot):
            blocks[s, k] = blocks[s, k] + blocks[s, slots[64 + k, j]]
        return 0

    lax.fori_loop(0, nslot, merge, 0)

    def forward_units(units):
        def one(i, _):
            half = choose(i, [u[0] for u in units])
            slot = choose(i, [u[1] for u in units])
            j, at = panel_of(slot), 4 * half
            x = gathered[half, slot]
            for q in range(4):
                placed = jnp.concatenate(
                    [
                        jnp.concatenate([blocks[slot, slots[at + 8 * d + s, j]] for s in range(4)], axis=1)
                        for d in (2 * q, 2 * q + 1)
                    ],
                    axis=0,
                )
                acc[:, 256 * q : 256 * q + 256] += lax.dot_general(
                    x, placed, CONTRACT_LAST, preferred_element_type=F32
                )
            return 0

        if units:
            lax.fori_loop(0, len(units), one, 0)

    forward_units(((0, 0), (1, 0)))
    def leaves_of(k):
        return [m for m in ROUNDS[k] if m in LEAVES] if k >= 0 else []

    def wait_leaves(leaves):
        for m in leaves:
            link_copy(m).wait_recv()

    def pass_leaves(leaves):
        for m in leaves:
            link_copy(m).start()

    last = len(ROUNDS) - 1
    behind = []
    for k, now in enumerate(ROUNDS):
        late = leaves_of(k - 2)
        units = [(m[0], m[3]) for m in now if m not in LEAVES]
        for piece in range(PIECES):
            for m in now:
                unless_leaf(m, lambda: gather_copy(m, piece).wait_recv())
            if k + 2 < len(ROUNDS):
                for m in ROUNDS[k + 2]:
                    unless_leaf(m, lambda: gather_copy(m, piece).start())
            if piece == 0:
                if late:
                    pl.when(off_diag)(lambda: wait_leaves(late))
                forward_units(behind + [(m[0], m[3]) for m in late])
        if leaves_of(k):
            pl.when(diag)(lambda: pass_leaves(leaves_of(k)))
        forward_units(units[:2])
        behind = units[2:]
        if k == 4:
            for other in (1, 2, 3):
                cot_landed(other).wait_recv()
                bias_copy(other, (col + 4 - other) % 4).wait_recv()
            for h in range(2):
                lanes = jnp.concatenate([bias_got[2 * h][0:1, :64], bias_got[2 * h + 1][0:1, :64]], axis=1)
                bias_col[h * 128 : h * 128 + 128, :] = jnp.broadcast_to(lanes, (128, 128)).T

    forward_units(behind)

    sibling = device(y, a, z, hi, 1 - b)
    peer = device(y, a, z, 1 - hi, b)
    own_rows = pl.ds(pl.multiple_of(hi * 128, 128), 128)
    peer_rows = pl.ds(pl.multiple_of(128 - hi * 128, 128), 128)

    def lanes(t):
        return pl.ds(t * 128, 128)

    def part_copy(t):
        theirs = pl.ds(pl.multiple_of((1 - b) * 512 + t * 128, 128), 128)
        return remote(acc.at[:, theirs], part_got.at[t], PART + t, PART + t, sibling)

    def agg_copy(t, rows):
        return remote(agg.at[own_rows, lanes(t)], agg.at[rows, lanes(t)], AGG + t, AGG + t, peer)

    def grad_copy(t, core):
        return remote(grad_agg.at[4 * b + t], grad_agg.at[4 * core + t], GRAD + t, GRAD + t, sibling)

    for t in range(4):
        part_copy(t).start()
    for t in range(4):
        part_copy(t).wait_recv()
        mine = pl.ds(pl.multiple_of(b * 512 + t * 128, 128), 128)
        agg[own_rows, lanes(t)] = (acc[:, mine] + part_got[t]).astype(BF)
        agg_copy(t, own_rows).start()
    for m in NUMBER:
        for piece in range(PIECES):
            unless_leaf(m, lambda: gather_copy(m, piece).wait_send())

    def links_sent(copy):
        for m in LEAVES:
            copy(m).wait_send()

    pl.when(diag)(lambda: links_sent(link_copy))
    for t in range(4):
        agg_copy(t, peer_rows).wait_recv()
        pre = jnp.dot(weight_t[...], agg[:, lanes(t)], preferred_element_type=F32) + bias_col[...]
        sig = jax.nn.sigmoid(pre)
        value = pre * sig
        grad = (cot_all[:, lanes(t)].astype(F32) * sig * (1.0 + pre * (1.0 - sig))).astype(BF)
        pre_grad[:, lanes(t)] = grad
        grad_agg[4 * b + t] = jnp.dot(weight[own_rows, :], grad, preferred_element_type=F32).astype(BF)
        grad_copy(t, b).start()
        out_half[:, lanes(t)] = jnp.where(hi == 0, value[:128], value[128:]).astype(BF)
    out_copy = remote(out_half.at[rows64(1 - b)], out_got, OUT, OUT, sibling)
    out_copy.start()

    term = lax.dot_general(agg[own_rows, :], pre_grad[...], CONTRACT_LAST, preferred_element_type=F32)
    bias_term = lax.dot_general(jnp.ones((16, 512), BF), pre_grad[...], CONTRACT_LAST, preferred_element_type=F32)
    for core in range(2):
        wterm[core, :64] = term[core * 64 : core * 64 + 64, :]
        wterm[core, 64:] = bias_term
    weight_core = remote(wterm.at[1 - b], wcore, WEIGHT, WEIGHT, sibling)
    weight_core.start()
    weight_link = remote(wlink.at[0], wlink.at[1], WEIGHT + 1, WEIGHT + 1, device(y, 1 - a, z, hi, b))

    def weight_y(k, place):
        return remote(
            wy.at[y], wy.at[place], WEIGHT + 1 + k, WEIGHT + 1 + k, device((y + k) % 4, a, z, hi, b)
        )

    def weight_z(k, place):
        return remote(
            wz.at[z], wz.at[place], WEIGHT + 4 + k, WEIGHT + 4 + k, device(y, a, (z + k) % 4, hi, b)
        )

    def scatter_copy(m, piece):
        half, way, start, end = m
        n = PIECES * NUMBER[m] + piece
        rows = pl.ds(piece * ROWS, ROWS)
        return pltpu.make_async_remote_copy(
            src_ref=shares.at[half, end, rows],
            dst_ref=shares_got.at[NUMBER[m], rows],
            send_sem=send_sem.at[n],
            recv_sem=scatter_sem.at[n],
            device_id=step((-way[0], -way[1])),
            device_id_type=MESH,
        )

    def link_share(m):
        n = LEAVES.index(m)
        return pltpu.make_async_remote_copy(
            src_ref=shares.at[m[0], m[3]],
            dst_ref=link_got.at[n],
            send_sem=link_send.at[n],
            recv_sem=link_back.at[n],
            device_id=device(y, 1 - a, z, hi, b),
            device_id_type=MESH,
        )

    def backward_units(units, result):
        def one(i, _):
            half = choose(i, [u[0] for u in units])
            slot = choose(i, [u[1] for u in units])
            j, at = panel_of(slot), 4 * half
            grads = jnp.concatenate([grad_agg[d] for d in range(8)], axis=1)
            for s in (0, 2):
                placed = jnp.concatenate(
                    [
                        jnp.concatenate([blocks[slot, slots[at + 8 * d + s + e, j]] for e in (0, 1)], axis=1)
                        for d in range(8)
                    ],
                    axis=0,
                )
                result[i, :, s * 128 : s * 128 + 256] = jnp.dot(
                    grads, placed, preferred_element_type=F32
                )
            return 0

        lax.fori_loop(0, len(units), one, 0)

    def add_up(half, slot, result, into, piece):
        came = [m for m in SENT_FROM.get((half, slot), ()) if m not in LEAVES]
        leaves = [m for m in SENT_FROM.get((half, slot), ()) if m in LEAVES]
        rows = slice(piece * ROWS, piece * ROWS + ROWS)

        def add_leaves():
            for m in leaves:
                scatter_copy(m, piece).wait_recv()
                result[rows, :] += shares_got[NUMBER[m], rows, :].astype(F32)

        if leaves:
            pl.when(diag)(add_leaves)
        for m in came:
            scatter_copy(m, piece).wait_recv()
        total = result[rows, :]
        for m in came:
            total = total + shares_got[NUMBER[m], rows, :].astype(F32)
        into[rows, :] = total.astype(BF)

    for t in range(4):
        grad_copy(t, 1 - b).wait_recv()
    def backward_leaves(k):
        leaves = [m for m in ROUNDS[k] if m in LEAVES]
        if leaves:
            first = LEAVES.index(leaves[0])
            backward_units([(m[0], m[3]) for m in leaves], leaf_part.at[pl.ds(first, len(leaves))])

            def give():
                for m in leaves:
                    shares[m[0], m[3]] = leaf_part[LEAVES.index(m)].astype(BF)
                    link_share(m).start()

            pl.when(off_diag)(give)

    def send_leaf(m):
        n = LEAVES.index(m)
        link_share(m).wait_recv()
        shares[m[0], m[3]] = (leaf_part[n] + link_got[n].astype(F32)).astype(BF)
        for piece in range(PIECES):
            scatter_copy(m, piece).start()

    for k in range(last, -1, -1):
        now = [m for m in ROUNDS[k] if m not in LEAVES]
        backward_units([(m[0], m[3]) for m in now], part)
        for piece in range(PIECES):
            for i, m in enumerate(now):
                add_up(m[0], m[3], part.at[i], shares.at[m[0], m[3]], piece)
                scatter_copy(m, piece).start()
        for m in ROUNDS[k]:
            if m in LEAVES:
                pl.when(diag)(lambda: send_leaf(m))
        if k >= 2:
            backward_leaves(k - 2)
        if k == 7:
            weight_core.wait_recv()
            wlink[0] = wterm[b] + wcore[...]
            weight_link.start()
        if k == 5:
            weight_link.wait_recv()
            wy[y] = (wlink[0] + wlink[1]).astype(BF)
            for n in (1, 2, 3):
                weight_y(n, y).start()
        if k == 2:
            for n in (1, 2, 3):
                weight_y(n, (y + 4 - n) % 4).wait_recv()
            wz[z] = sum(wy[n].astype(F32) for n in range(4)).astype(BF)
            for n in (1, 2, 3):
                weight_z(n, z).start()

    backward_units(((0, 0), (1, 0)), own_part)
    out_copy.wait_recv()
    for half in range(2):
        at = slice(half * 512, half * 512 + 512)
        out_ref[:, at] = jnp.where(b == half, out_half[rows64(b), :], out_got[...])

    def final_copy(half, core, chip_from, target):
        lane = pl.ds(half * 512, 512)
        return remote(
            final.at[half, pl.ds(core * 64, 64)],
            final_got.at[chip_from, :, lane],
            FINAL + 2 * half + core,
            FINAL + 2 * half + chip_from,
            target,
        )

    for half in (1, 0):
        for piece in range(PIECES):
            add_up(half, 0, own_part.at[half], final.at[half], piece)
        for core in range(2):
            here = jnp.logical_and(a == b, b == core)

            @pl.when(jnp.logical_not(here))
            def _():
                final_copy(half, core, a, device(y, b, z, hi, core)).start()

            @pl.when(here)
            def _():
                final_got[a, :, half * 512 : half * 512 + 512] = final[half, core * 64 : core * 64 + 64, :]

    for half in range(2):
        for chip in range(2):

            @pl.when(jnp.logical_not(jnp.logical_and(a == chip, a == b)))
            def _():
                feature_copy(half, chip, b, device(y, chip, z, hi, a)).wait_send()

            @pl.when(jnp.logical_not(jnp.logical_and(a == b, b == chip)))
            def _():
                final_copy(half, chip, a, device(y, b, z, hi, chip)).wait_send()

    for k in (1, 2, 3):
        cot_copy(k).wait_send()
        bias_copy(k, col).wait_send()
        weight_y(k, y).wait_send()
        weight_z(k, z).wait_send()
    for t in range(4):
        part_copy(t).wait_send()
        agg_copy(t, own_rows).wait_send()
        grad_copy(t, b).wait_send()
    out_copy.wait_send()
    weight_core.wait_send()
    weight_link.wait_send()
    for m in NUMBER:
        for piece in range(PIECES):
            unless_leaf(m, lambda: scatter_copy(m, piece).wait_send())
    pl.when(off_diag)(lambda: links_sent(link_share))

    for n in (1, 2, 3):
        weight_z(n, (z + 4 - n) % 4).wait_recv()
    scale = 1.0 / (32 * 1024) ** 0.5
    whole = sum(wz[n].astype(F32) for n in range(4)) * scale
    gw_ref[...] = whole[:64, :]
    gb = whole[64:65, :]
    own = jnp.where(hi == 0, gb[:, :128], gb[:, 128:])
    gb_ref[...] = jnp.where(b == 0, own[:, :64], own[:, 64:])

    for half in (1, 0):
        for chip in range(2):

            @pl.when(jnp.logical_not(jnp.logical_and(a == b, chip == a)))
            def _():
                final_copy(half, 0, chip, device(y, 1 - a, z, hi, b)).wait_recv()

        at = slice(half * 512, half * 512 + 512)
        gin_ref[:, at] = (final_got[0, :, at].astype(F32) + final_got[1, :, at].astype(F32)).astype(BF)


def hand_over(*refs):
    half = len(refs) // 2
    for n in range(half):
        refs[half + n][...] = refs[n][...]


def body(features, weight, bias, edge_blocks, block_dst, block_src, counts, cotangent):
    vmem = pl.BlockSpec(memory_space=pltpu.VMEM)
    out, gin, gw, gb = pl.pallas_call(
        kernel,
        out_shape=(
            jax.ShapeDtypeStruct((64, 1024), BF),
            jax.ShapeDtypeStruct((64, 1024), BF),
            jax.ShapeDtypeStruct((64, 256), F32),
            jax.ShapeDtypeStruct((1, 64), F32),
        ),
        in_specs=[vmem, vmem, vmem, vmem, vmem, vmem, vmem, pl.BlockSpec(memory_space=pl.ANY)],
        out_specs=(vmem, vmem, vmem, vmem),
        scratch_shapes=[
            pltpu.VMEM((16, 17, 128, 128), BF),
            pltpu.VMEM((2, 16, 128, 512), BF),
            pltpu.VMEM((128, 1024), F32),
            pltpu.VMEM((256, 512), BF),
            pltpu.VMEM((4, 8, 128), F32),
            pltpu.VMEM((256, 128), F32),
            pltpu.VMEM((256, 256), BF),
            pltpu.VMEM((4, 128, 128), F32),
            pltpu.VMEM((256, 512), BF),
            pltpu.VMEM((256, 512), BF),
            pltpu.VMEM((8, 128, 128), BF),
            pltpu.VMEM((128, 512), BF),
            pltpu.VMEM((64, 512), BF),
            pltpu.VMEM((2, 80, 256), F32),
            pltpu.VMEM((80, 256), F32),
            pltpu.VMEM((2, 80, 256), F32),
            pltpu.VMEM((4, 80, 256), BF),
            pltpu.VMEM((4, 80, 256), BF),
            pltpu.VMEM((4, 128, 512), F32),
            pltpu.VMEM((2, 128, 512), F32),
            pltpu.VMEM((2, 16, 128, 512), BF),
            pltpu.VMEM((MESSAGES, 128, 512), BF),
            pltpu.VMEM((2, 128, 512), BF),
            pltpu.VMEM((2, 64, 1024), BF),
            pltpu.VMEM((80, 128), jnp.int32),
            pltpu.SMEM((80, 128), jnp.int32),
            pltpu.VMEM((len(LEAVES), 128, 512), BF),
            pltpu.VMEM((len(LEAVES), 128, 512), F32),
            pltpu.SemaphoreType.DMA,
            pltpu.SemaphoreType.DMA((len(LEAVES),)),
            pltpu.SemaphoreType.DMA((len(LEAVES),)),
            pltpu.SemaphoreType.DMA((len(LEAVES),)),
            pltpu.SemaphoreType.DMA((16,)),
            pltpu.SemaphoreType.DMA((PIECES * MESSAGES,)),
            pltpu.SemaphoreType.DMA((PIECES * MESSAGES,)),
            pltpu.SemaphoreType.DMA((PIECES * MESSAGES,)),
            pltpu.SemaphoreType.DMA((END,)),
            pltpu.SemaphoreType.DMA((END,)),
        ],
        compiler_params=pltpu.CompilerParams(
            collective_id=0, has_side_effects=True, vmem_limit_bytes=56 * 1024 * 1024
        ),
        name="graph_layer",
    )(block_dst[0].T, block_src[0].T, counts, features.T, cotangent.T, weight, bias.reshape(1, 64), edge_blocks[0])
    results = (out, gin, gw, gb)
    out, gin, gw, gb = pl.pallas_call(
        hand_over,
        out_shape=tuple(jax.ShapeDtypeStruct(x.shape, x.dtype) for x in results),
        in_specs=[vmem] * 4,
        out_specs=(vmem,) * 4,
        name="hand_over",
    )(*results)
    return out.T, gin.T, gw, gb.reshape(64)


def solution(mesh):
    return jax.shard_map(
        body,
        mesh=mesh,
        in_specs=(
            P("row", "col"),
            P(),
            P("col"),
            P("row", None, None, None, None),
            P("row", None, None),
            P("row", None, None),
            P("row", None),
            P("row", "col"),
        ),
        out_specs=(P("row", "col"), P("row", "col"), P("col", None), P("col")),
        check_vma=False,
    )
```

```python
import functools

import jax
import jax.numpy as jnp
from jax import lax
from jax.experimental import pallas as pl
from jax.experimental.pallas import tpu as pltpu
from jax.sharding import PartitionSpec as P

MESH = pl.DeviceIdType.MESH
BF = jnp.bfloat16
F32 = jnp.float32

YP, YM, ZP, ZM = (1, 0), (-1, 0), (0, 1), (0, -1)


def _message(half, way, dy, dz):
    return (half, way, 4 * dy + dz, 4 * ((dy - way[0]) % 4) + (dz - way[1]) % 4)


ROUNDS = (
    (_message(0, YP, 0, 0), _message(0, YM, 0, 0), _message(0, ZP, 0, 0), _message(0, ZM, 0, 0)),
    (_message(1, ZP, 0, 0), _message(1, ZM, 0, 0), _message(1, YP, 0, 0), _message(1, YM, 0, 0)),
    (_message(0, YP, 3, 0), _message(0, ZP, 1, 0), _message(0, ZM, 1, 0)),
    (_message(1, YP, 0, 1), _message(1, YM, 0, 1), _message(1, ZP, 0, 3), _message(0, ZM, 3, 0)),
    (_message(1, YP, 0, 3), _message(1, YM, 0, 3), _message(0, ZP, 3, 0), _message(0, ZM, 2, 0)),
    (_message(1, YP, 0, 2), _message(1, YM, 0, 2), _message(0, ZP, 2, 0), _message(0, ZM, 1, 1)),
    (_message(1, YP, 3, 0), _message(1, YM, 1, 1), _message(0, ZP, 0, 3), _message(0, ZM, 3, 1)),
    (_message(1, YP, 3, 2), _message(1, YM, 1, 3), _message(0, ZP, 2, 3)),
)
NUMBER = {}
for _round in ROUNDS:
    for _m in _round:
        NUMBER[_m] = len(NUMBER)
MESSAGES = len(NUMBER)
PIECES = 2
ROWS = 128 // PIECES
SENT_FROM = {}
for _m in NUMBER:
    SENT_FROM.setdefault((_m[0], _m[2]), []).append(_m)

LEAVES = tuple(
    m
    for now in ROUNDS[:6]
    for m in now
    if (m[0], m[3]) not in SENT_FROM and m != _message(0, ZM, 1, 1)
)
FEAT, COT, BIAS, PART, AGG, GRAD, OUT, WEIGHT, FINAL, END = 0, 4, 7, 10, 14, 18, 22, 23, 31, 35
CONTRACT_LAST = (((1,), (1,)), ((), ()))


def choose(i, values):
    chosen = jnp.int32(values[0])
    for n, value in enumerate(values[1:], 1):
        chosen = jnp.where(i == n, jnp.int32(value), chosen)
    return chosen


def kernel(
    dst_ids,
    src_ids,
    counts,
    feat,
    cot,
    weight,
    bias,
    edge,
    out_ref,
    gin_ref,
    gw_ref,
    gb_ref,
    blocks,
    gathered,
    acc,
    cot_all,
    bias_got,
    bias_col,
    weight_t,
    part_got,
    agg,
    pre_grad,
    grad_agg,
    out_half,
    out_got,
    wterm,
    wcore,
    wlink,
    wy,
    wz,
    part,
    own_part,
    shares,
    shares_got,
    final,
    final_got,
    lists,
    slots,
    link_got,
    leaf_part,
    list_sem,
    link_send,
    link_recv,
    link_back,
    edge_sem,
    send_sem,
    gather_sem,
    scatter_sem,
    odd_send,
    odd_recv,
):
    row, col = lax.axis_index("row"), lax.axis_index("col")
    y, a, z = row // 8, (row // 4) % 2, row % 4
    hi, b = col // 2, col % 2
    nslot = 16
    diag = a == b
    off_diag = jnp.logical_not(diag)

    def unless_leaf(m, run):
        if m in LEAVES:
            pl.when(diag)(run)
        else:
            run()


    def device(yy, aa, zz, hh, bb):
        return ((yy * 2 + aa) * 4 + zz, hh * 2 + bb)

    def step(way):
        return device((y + way[0] + 4) % 4, a, (z + way[1] + 4) % 4, hi, b)

    def panel_of(slot):
        return (((y + slot // 4) % 4) * 2 + b) * 4 + (z + slot % 4) % 4

    def rows64(core):
        return pl.ds(pl.multiple_of(core * 64, 64), 64)

    def remote(src, dst, n_send, n_recv, target):
        return pltpu.make_async_remote_copy(
            src_ref=src,
            dst_ref=dst,
            send_sem=odd_send.at[n_send],
            recv_sem=odd_recv.at[n_recv],
            device_id=target,
            device_id_type=MESH,
        )

    partners = [device(y, 1 - a, z, hi, b), device(y, a, z, hi, 1 - b), device(y, 1 - a, z, hi, 1 - b)]
    partners += [device(y, a, z, 1 - hi, 0), device(y, a, z, 1 - hi, 1)]
    partners += [device((y + k) % 4, a, z, hi, b) for k in (1, 2, 3)]
    partners += [device(y, a, (z + k) % 4, hi, b) for k in (1, 2, 3)]
    barrier = pltpu.get_barrier_semaphore()
    for partner in partners:
        pl.semaphore_signal(barrier, inc=1, device_id=partner, device_id_type=MESH)

    loads = [
        pltpu.make_async_copy(
            edge.at[panel_of(s)], blocks.at[s, pl.ds(0, nslot)], edge_sem.at[s]
        )
        for s in range(nslot)
    ]
    for load in loads:
        load.start()

    k_of = lax.broadcasted_iota(jnp.int32, (nslot, 32), 0)
    cell = jnp.where(k_of < counts[...], dst_ids[...] * 8 + src_ids[...], -1)
    place = lax.broadcasted_iota(jnp.int32, (64, 32), 0)
    found = jnp.full((64, 32), nslot, jnp.int32)
    before = jnp.full((nslot, 32), nslot, jnp.int32)
    for k in range(nslot):
        before = jnp.where((cell == cell[k : k + 1, :]) & (k_of > k) & (cell >= 0), k, before)
        found = jnp.where(place == cell[k : k + 1, :], k, found)
    lists[...] = jnp.zeros_like(lists)
    lists[:64, :32] = found
    lists[64:, :32] = before
    list_copy = pltpu.make_async_copy(lists, slots, list_sem)
    list_copy.start()

    bias_row = bias[...]
    bias_got[col] = jnp.broadcast_to(jnp.concatenate([bias_row, bias_row], axis=1), (8, 128))
    pl.semaphore_wait(barrier, len(partners))

    def feature_copy(half, chip, core_from, target):
        return remote(
            feat.at[:, pl.ds(half * 512, 512)],
            gathered.at[half, 0, rows64(core_from)],
            FEAT + 2 * half + chip,
            FEAT + 2 * half + core_from,
            target,
        )

    for half in range(2):
        for chip in range(2):
            here = jnp.logical_and(a == chip, a == b)

            @pl.when(jnp.logical_not(here))
            def _():
                feature_copy(half, chip, b, device(y, chip, z, hi, a)).start()

            @pl.when(here)
            def _():
                gathered[half, 0, rows64(b), :] = feat[:, half * 512 : half * 512 + 512]

    def feature_landed(half):
        for core in range(2):

            @pl.when(jnp.logical_not(jnp.logical_and(a == b, core == b)))
            def _():
                feature_copy(half, 0, core, device(y, 1 - a, z, hi, b)).wait_recv()

    def gather_copy(m, piece):
        half, way, start, end = m
        n = PIECES * NUMBER[m] + piece
        rows = pl.ds(piece * ROWS, ROWS)
        return pltpu.make_async_remote_copy(
            src_ref=gathered.at[half, start, rows],
            dst_ref=gathered.at[half, end, rows],
            send_sem=send_sem.at[n],
            recv_sem=gather_sem.at[n],
            device_id=step(way),
            device_id_type=MESH,
        )

    def link_copy(m):
        n = LEAVES.index(m)
        return pltpu.make_async_remote_copy(
            src_ref=gathered.at[m[0], m[3]],
            dst_ref=gathered.at[m[0], m[3]],
            send_sem=link_send.at[n],
            recv_sem=link_recv.at[n],
            device_id=device(y, 1 - a, z, hi, b),
            device_id_type=MESH,
        )

    def cot_copy(k):
        other = (col + k) % 4
        return remote(
            cot.at[:, pl.ds(pl.multiple_of((other % 2) * 512, 512), 512)],
            cot_all.at[rows64(col)],
            COT + k - 1,
            COT + k - 1,
            (row, other),
        )

    def cot_landed(k):
        return remote(
            cot.at[:, pl.ds(0, 512)],
            cot_all.at[rows64((col + 4 - k) % 4)],
            COT + k - 1,
            COT + k - 1,
            (row, (col + k) % 4),
        )

    def bias_copy(k, place):
        return remote(bias_got.at[col], bias_got.at[place], BIAS + k - 1, BIAS + k - 1, (row, (col + k) % 4))

    acc[...] = jnp.zeros_like(acc)
    weight_t[...] = weight[...].T
    for half in range(2):
        feature_landed(half)
        for piece in range(PIECES):
            for m in ROUNDS[half]:
                unless_leaf(m, lambda: gather_copy(m, piece).start())
    for k in (1, 2, 3):
        cot_copy(k).start()
        bias_copy(k, col).start()
    cot_all[rows64(col), :] = cot[:, pl.ds(pl.multiple_of(b * 512, 512), 512)]

    list_copy.wait()
    for load in loads:
        load.wait()

    def merge(s, _):
        j = panel_of(s)
        blocks[s, nslot] = jnp.zeros((128, 128), BF)
        for k in range(1, nslot):
            blocks[s, k] = blocks[s, k] + blocks[s, slots[64 + k, j]]
        return 0

    lax.fori_loop(0, nslot, merge, 0)

    def forward_units(units):
        def one(i, _):
            half = choose(i, [u[0] for u in units])
            slot = choose(i, [u[1] for u in units])
            j, at = panel_of(slot), 4 * half
            x = gathered[half, slot]
            for q in range(4):
                placed = jnp.concatenate(
                    [
                        jnp.concatenate([blocks[slot, slots[at + 8 * d + s, j]] for s in range(4)], axis=1)
                        for d in (2 * q, 2 * q + 1)
                    ],
                    axis=0,
                )
                acc[:, 256 * q : 256 * q + 256] += lax.dot_general(
                    x, placed, CONTRACT_LAST, preferred_element_type=F32
                )
            return 0

        if units:
            lax.fori_loop(0, len(units), one, 0)

    def leaves_of(k):
        return [m for m in ROUNDS[k] if m in LEAVES] if k >= 0 else []

    def wait_leaves(leaves):
        for m in leaves:
            link_copy(m).wait_recv()

    def pass_leaves(leaves):
        for m in leaves:
            link_copy(m).start()

    last = len(ROUNDS) - 1
    behind = [(0, 0), (1, 0)]
    for k, now in enumerate(ROUNDS):
        late = leaves_of(k - 2)
        units = [(m[0], m[3]) for m in now if m not in LEAVES]
        for piece in range(PIECES):
            for m in now:
                unless_leaf(m, lambda: gather_copy(m, piece).wait_recv())
            if k + 2 < len(ROUNDS):
                for m in ROUNDS[k + 2]:
                    unless_leaf(m, lambda: gather_copy(m, piece).start())
            if piece == 0:
                if late:
                    pl.when(off_diag)(lambda: wait_leaves(late))
                forward_units(behind + [(m[0], m[3]) for m in late])
        if leaves_of(k):
            pl.when(diag)(lambda: pass_leaves(leaves_of(k)))
        forward_units(units[:2])
        behind = units[2:]
        if k == 4:
            for other in (1, 2, 3):
                cot_landed(other).wait_recv()
                bias_copy(other, (col + 4 - other) % 4).wait_recv()
            for h in range(2):
                lanes = jnp.concatenate([bias_got[2 * h][0:1, :64], bias_got[2 * h + 1][0:1, :64]], axis=1)
                bias_col[h * 128 : h * 128 + 128, :] = jnp.broadcast_to(lanes, (128, 128)).T

    forward_units(behind)

    sibling = device(y, a, z, hi, 1 - b)
    peer = device(y, a, z, 1 - hi, b)
    own_rows = pl.ds(pl.multiple_of(hi * 128, 128), 128)
    peer_rows = pl.ds(pl.multiple_of(128 - hi * 128, 128), 128)

    def lanes(t):
        return pl.ds(t * 128, 128)

    def part_copy(t):
        theirs = pl.ds(pl.multiple_of((1 - b) * 512 + t * 128, 128), 128)
        return remote(acc.at[:, theirs], part_got.at[t], PART + t, PART + t, sibling)

    def agg_copy(t, rows):
        return remote(agg.at[own_rows, lanes(t)], agg.at[rows, lanes(t)], AGG + t, AGG + t, peer)

    def grad_copy(t, core):
        return remote(grad_agg.at[4 * b + t], grad_agg.at[4 * core + t], GRAD + t, GRAD + t, sibling)

    for t in range(4):
        part_copy(t).start()
    for t in range(4):
        part_copy(t).wait_recv()
        mine = pl.ds(pl.multiple_of(b * 512 + t * 128, 128), 128)
        agg[own_rows, lanes(t)] = (acc[:, mine] + part_got[t]).astype(BF)
        agg_copy(t, own_rows).start()
    for m in NUMBER:
        for piece in range(PIECES):
            unless_leaf(m, lambda: gather_copy(m, piece).wait_send())

    def links_sent(copy):
        for m in LEAVES:
            copy(m).wait_send()

    pl.when(diag)(lambda: links_sent(link_copy))
    for t in range(4):
        agg_copy(t, peer_rows).wait_recv()
        pre = jnp.dot(weight_t[...], agg[:, lanes(t)], preferred_element_type=F32) + bias_col[...]
        sig = jax.nn.sigmoid(pre)
        value = pre * sig
        grad = (cot_all[:, lanes(t)].astype(F32) * sig * (1.0 + pre * (1.0 - sig))).astype(BF)
        pre_grad[:, lanes(t)] = grad
        grad_agg[4 * b + t] = jnp.dot(weight[own_rows, :], grad, preferred_element_type=F32).astype(BF)
        grad_copy(t, b).start()
        out_half[:, lanes(t)] = jnp.where(hi == 0, value[:128], value[128:]).astype(BF)
    out_copy = remote(out_half.at[rows64(1 - b)], out_got, OUT, OUT, sibling)
    out_copy.start()

    term = lax.dot_general(agg[own_rows, :], pre_grad[...], CONTRACT_LAST, preferred_element_type=F32)
    bias_term = lax.dot_general(jnp.ones((16, 512), BF), pre_grad[...], CONTRACT_LAST, preferred_element_type=F32)
    for core in range(2):
        wterm[core, :64] = term[core * 64 : core * 64 + 64, :]
        wterm[core, 64:] = bias_term
    weight_core = remote(wterm.at[1 - b], wcore, WEIGHT, WEIGHT, sibling)
    weight_core.start()
    weight_link = remote(wlink.at[0], wlink.at[1], WEIGHT + 1, WEIGHT + 1, device(y, 1 - a, z, hi, b))

    def weight_y(k, place):
        return remote(
            wy.at[y], wy.at[place], WEIGHT + 1 + k, WEIGHT + 1 + k, device((y + k) % 4, a, z, hi, b)
        )

    def weight_z(k, place):
        return remote(
            wz.at[z], wz.at[place], WEIGHT + 4 + k, WEIGHT + 4 + k, device(y, a, (z + k) % 4, hi, b)
        )

    def scatter_copy(m, piece):
        half, way, start, end = m
        n = PIECES * NUMBER[m] + piece
        rows = pl.ds(piece * ROWS, ROWS)
        return pltpu.make_async_remote_copy(
            src_ref=shares.at[half, end, rows],
            dst_ref=shares_got.at[NUMBER[m], rows],
            send_sem=send_sem.at[n],
            recv_sem=scatter_sem.at[n],
            device_id=step((-way[0], -way[1])),
            device_id_type=MESH,
        )

    def link_share(m):
        n = LEAVES.index(m)
        return pltpu.make_async_remote_copy(
            src_ref=shares.at[m[0], m[3]],
            dst_ref=link_got.at[n],
            send_sem=link_send.at[n],
            recv_sem=link_back.at[n],
            device_id=device(y, 1 - a, z, hi, b),
            device_id_type=MESH,
        )

    def backward_units(units, result):
        def one(i, _):
            half = choose(i, [u[0] for u in units])
            slot = choose(i, [u[1] for u in units])
            j, at = panel_of(slot), 4 * half
            grads = jnp.concatenate([grad_agg[d] for d in range(8)], axis=1)
            for s in (0, 2):
                placed = jnp.concatenate(
                    [
                        jnp.concatenate([blocks[slot, slots[at + 8 * d + s + e, j]] for e in (0, 1)], axis=1)
                        for d in range(8)
                    ],
                    axis=0,
                )
                result[i, :, s * 128 : s * 128 + 256] = jnp.dot(
                    grads, placed, preferred_element_type=F32
                )
            return 0

        lax.fori_loop(0, len(units), one, 0)

    def add_up(half, slot, result, into, piece):
        came = [m for m in SENT_FROM.get((half, slot), ()) if m not in LEAVES]
        leaves = [m for m in SENT_FROM.get((half, slot), ()) if m in LEAVES]
        rows = slice(piece * ROWS, piece * ROWS + ROWS)

        def add_leaves():
            for m in leaves:
                scatter_copy(m, piece).wait_recv()
                result[rows, :] += shares_got[NUMBER[m], rows, :].astype(F32)

        if leaves:
            pl.when(diag)(add_leaves)
        for m in came:
            scatter_copy(m, piece).wait_recv()
        total = result[rows, :]
        for m in came:
            total = total + shares_got[NUMBER[m], rows, :].astype(F32)
        into[rows, :] = total.astype(BF)

    for t in range(4):
        grad_copy(t, 1 - b).wait_recv()
    def backward_leaves(k):
        leaves = [m for m in ROUNDS[k] if m in LEAVES]
        if leaves:
            first = LEAVES.index(leaves[0])
            backward_units([(m[0], m[3]) for m in leaves], leaf_part.at[pl.ds(first, len(leaves))])

            def give():
                for m in leaves:
                    shares[m[0], m[3]] = leaf_part[LEAVES.index(m)].astype(BF)
                    link_share(m).start()

            pl.when(off_diag)(give)

    def send_leaf(m):
        n = LEAVES.index(m)
        link_share(m).wait_recv()
        shares[m[0], m[3]] = (leaf_part[n] + link_got[n].astype(F32)).astype(BF)
        for piece in range(PIECES):
            scatter_copy(m, piece).start()

    for k in range(last, -1, -1):
        now = [m for m in ROUNDS[k] if m not in LEAVES]
        backward_units([(m[0], m[3]) for m in now], part)
        for piece in range(PIECES):
            for i, m in enumerate(now):
                add_up(m[0], m[3], part.at[i], shares.at[m[0], m[3]], piece)
                scatter_copy(m, piece).start()
        for m in ROUNDS[k]:
            if m in LEAVES:
                pl.when(diag)(lambda: send_leaf(m))
        if k >= 2:
            backward_leaves(k - 2)
        if k == 7:
            weight_core.wait_recv()
            wlink[0] = wterm[b] + wcore[...]
            weight_link.start()
        if k == 5:
            weight_link.wait_recv()
            wy[y] = (wlink[0] + wlink[1]).astype(BF)
            for n in (1, 2, 3):
                weight_y(n, y).start()
        if k == 3:
            for n in (1, 2, 3):
                weight_y(n, (y + 4 - n) % 4).wait_recv()
            wz[z] = sum(wy[n].astype(F32) for n in range(4)).astype(BF)
            for n in (1, 2, 3):
                weight_z(n, z).start()

    backward_units(((0, 0), (1, 0)), own_part)
    out_copy.wait_recv()
    for half in range(2):
        at = slice(half * 512, half * 512 + 512)
        out_ref[:, at] = jnp.where(b == half, out_half[rows64(b), :], out_got[...])

    def final_copy(half, core, chip_from, target):
        lane = pl.ds(half * 512, 512)
        return remote(
            final.at[half, pl.ds(core * 64, 64)],
            final_got.at[chip_from, :, lane],
            FINAL + 2 * half + core,
            FINAL + 2 * half + chip_from,
            target,
        )

    for half in (1, 0):
        for piece in range(PIECES):
            add_up(half, 0, own_part.at[half], final.at[half], piece)
        for core in range(2):
            here = jnp.logical_and(a == b, b == core)

            @pl.when(jnp.logical_not(here))
            def _():
                final_copy(half, core, a, device(y, b, z, hi, core)).start()

            @pl.when(here)
            def _():
                final_got[a, :, half * 512 : half * 512 + 512] = final[half, core * 64 : core * 64 + 64, :]

    for half in range(2):
        for chip in range(2):

            @pl.when(jnp.logical_not(jnp.logical_and(a == chip, a == b)))
            def _():
                feature_copy(half, chip, b, device(y, chip, z, hi, a)).wait_send()

            @pl.when(jnp.logical_not(jnp.logical_and(a == b, b == chip)))
            def _():
                final_copy(half, chip, a, device(y, b, z, hi, chip)).wait_send()

    for k in (1, 2, 3):
        cot_copy(k).wait_send()
        bias_copy(k, col).wait_send()
        weight_y(k, y).wait_send()
        weight_z(k, z).wait_send()
    for t in range(4):
        part_copy(t).wait_send()
        agg_copy(t, own_rows).wait_send()
        grad_copy(t, b).wait_send()
    out_copy.wait_send()
    weight_core.wait_send()
    weight_link.wait_send()
    for m in NUMBER:
        for piece in range(PIECES):
            unless_leaf(m, lambda: scatter_copy(m, piece).wait_send())
    pl.when(off_diag)(lambda: links_sent(link_share))

    for n in (1, 2, 3):
        weight_z(n, (z + 4 - n) % 4).wait_recv()
    scale = 1.0 / (32 * 1024) ** 0.5
    whole = sum(wz[n].astype(F32) for n in range(4)) * scale
    gw_ref[...] = whole[:64, :]
    gb = whole[64:65, :]
    own = jnp.where(hi == 0, gb[:, :128], gb[:, 128:])
    gb_ref[...] = jnp.where(b == 0, own[:, :64], own[:, 64:])

    for half in (1, 0):
        for chip in range(2):

            @pl.when(jnp.logical_not(jnp.logical_and(a == b, chip == a)))
            def _():
                final_copy(half, 0, chip, device(y, 1 - a, z, hi, b)).wait_recv()

        at = slice(half * 512, half * 512 + 512)
        gin_ref[:, at] = (final_got[0, :, at].astype(F32) + final_got[1, :, at].astype(F32)).astype(BF)


def hand_over(*refs):
    half = len(refs) // 2
    for n in range(half):
        refs[half + n][...] = refs[n][...]


def body(features, weight, bias, edge_blocks, block_dst, block_src, counts, cotangent):
    vmem = pl.BlockSpec(memory_space=pltpu.VMEM)
    out, gin, gw, gb = pl.pallas_call(
        kernel,
        out_shape=(
            jax.ShapeDtypeStruct((64, 1024), BF),
            jax.ShapeDtypeStruct((64, 1024), BF),
            jax.ShapeDtypeStruct((64, 256), F32),
            jax.ShapeDtypeStruct((1, 64), F32),
        ),
        in_specs=[vmem, vmem, vmem, vmem, vmem, vmem, vmem, pl.BlockSpec(memory_space=pl.ANY)],
        out_specs=(vmem, vmem, vmem, vmem),
        scratch_shapes=[
            pltpu.VMEM((16, 17, 128, 128), BF),
            pltpu.VMEM((2, 16, 128, 512), BF),
            pltpu.VMEM((128, 1024), F32),
            pltpu.VMEM((256, 512), BF),
            pltpu.VMEM((4, 8, 128), F32),
            pltpu.VMEM((256, 128), F32),
            pltpu.VMEM((256, 256), BF),
            pltpu.VMEM((4, 128, 128), F32),
            pltpu.VMEM((256, 512), BF),
            pltpu.VMEM((256, 512), BF),
            pltpu.VMEM((8, 128, 128), BF),
            pltpu.VMEM((128, 512), BF),
            pltpu.VMEM((64, 512), BF),
            pltpu.VMEM((2, 80, 256), F32),
            pltpu.VMEM((80, 256), F32),
            pltpu.VMEM((2, 80, 256), F32),
            pltpu.VMEM((4, 80, 256), BF),
            pltpu.VMEM((4, 80, 256), BF),
            pltpu.VMEM((4, 128, 512), F32),
            pltpu.VMEM((2, 128, 512), F32),
            pltpu.VMEM((2, 16, 128, 512), BF),
            pltpu.VMEM((MESSAGES, 128, 512), BF),
            pltpu.VMEM((2, 128, 512), BF),
            pltpu.VMEM((2, 64, 1024), BF),
            pltpu.VMEM((80, 128), jnp.int32),
            pltpu.SMEM((80, 128), jnp.int32),
            pltpu.VMEM((len(LEAVES), 128, 512), BF),
            pltpu.VMEM((len(LEAVES), 128, 512), F32),
            pltpu.SemaphoreType.DMA,
            pltpu.SemaphoreType.DMA((len(LEAVES),)),
            pltpu.SemaphoreType.DMA((len(LEAVES),)),
            pltpu.SemaphoreType.DMA((len(LEAVES),)),
            pltpu.SemaphoreType.DMA((16,)),
            pltpu.SemaphoreType.DMA((PIECES * MESSAGES,)),
            pltpu.SemaphoreType.DMA((PIECES * MESSAGES,)),
            pltpu.SemaphoreType.DMA((PIECES * MESSAGES,)),
            pltpu.SemaphoreType.DMA((END,)),
            pltpu.SemaphoreType.DMA((END,)),
        ],
        compiler_params=pltpu.CompilerParams(
            collective_id=0, has_side_effects=True, vmem_limit_bytes=56 * 1024 * 1024
        ),
        name="graph_layer",
    )(block_dst[0].T, block_src[0].T, counts, features.T, cotangent.T, weight, bias.reshape(1, 64), edge_blocks[0])
    results = (out, gin, gw, gb)
    out, gin, gw, gb = pl.pallas_call(
        hand_over,
        out_shape=tuple(jax.ShapeDtypeStruct(x.shape, x.dtype) for x in results),
        in_specs=[vmem] * 4,
        out_specs=(vmem,) * 4,
        name="hand_over",
    )(*results)
    return out.T, gin.T, gw, gb.reshape(64)


def solution(mesh):
    return jax.shard_map(
        body,
        mesh=mesh,
        in_specs=(
            P("row", "col"),
            P(),
            P("col"),
            P("row", None, None, None, None),
            P("row", None, None),
            P("row", None, None),
            P("row", None),
            P("row", "col"),
        ),
        out_specs=(P("row", "col"), P("row", "col"), P("col", None), P("col")),
        check_vma=False,
    )
```
